32 devices in a mesh: section: 2 (over x), frames: 4 (over y, core), space: 4 (over z).
Axes of the slice: x: 2, y: 2, z: 4, core: 2. Of those that a mesh axis runs over, the one named last changes fastest.
Arguments:
- base_frames: bfloat16 [8, 32, 32, 8, 128], P(None, 'frames', 'space'), may hold values from -6 to 6
- section_noise: bfloat16 [2, 8, 32, 32, 8, 128], P('section', None, 'frames', 'space'), may hold values from -6 to 6
- noise_levels: bfloat16 [2], P('section'), may hold values from 0.29882812 to 1
- spatial_kernel: bfloat16 [2, 9, 128, 128], P('section'), may hold values from -0.15625 to 0.15625
- temporal_kernel: bfloat16 [2, 3, 128, 128], P('section'), may hold values from -0.15625 to 0.15625
- output_weight: bfloat16 [2, 128, 128], P('section'), may hold values from -0.5 to 0.5
Outputs:
- denoised: bfloat16 [2, 8, 32, 32, 8, 128], P('section', None, 'frames', 'space')
The draws below stay inside these ranges and needn't reach their ends.
All inputs are finite; a program needn't handle non-finite values.
Results may differ from the reference program's by a relative error of at most 0.008.
Values may be sent and summed in bfloat16 or wider, within the bound.
A program may use at most 64 MiB of HBM per device.

```python
import math
import jax
import jax.numpy as jnp
from jax import lax

C = 128
VIDEOS = 8
COLS = 8
SECTIONS = 2
FRAMES = 32
ROWS = 32


def steps_of(rng, dims, cuts, low, top_value):
    loudness = 1.0
    for dim, blocks in cuts:
        heights = jax.random.uniform(jax.random.fold_in(jax.random.fold_in(rng, 6), dim), (blocks,), jnp.float32, low / len(cuts), top_value / len(cuts))
        loudness = loudness * jnp.repeat(jnp.exp(heights), dims[dim] // blocks).reshape((-1,) + (1,) * (len(dims) - 1 - dim))
    return loudness


def normal_values(stream_key, extent, width, reach, pieces=(), dtype=jnp.bfloat16):
    drawn = jax.random.normal(stream_key, extent, jnp.float32) * width
    if len(pieces) > 0:
        drawn = steps_of(stream_key, extent, pieces, -0.22, 0.18) * drawn
    return jnp.clip(drawn, min=-reach, max=reach).astype(dtype)


def setup_inputs(seed: int = 0) -> dict:
    splits = jax.random.split(jax.random.key(seed), 7)
    return {
        "base_frames": normal_values(splits[0], (VIDEOS, FRAMES, ROWS, COLS, C), 1.0, 6.0, ((1, 4), (2, 4))),
        "section_noise": normal_values(splits[1], (SECTIONS, VIDEOS, FRAMES, ROWS, COLS, C), 1.0, 6.0, ((0, 2), (2, 4), (3, 4))),
        "noise_levels": jnp.clip(jnp.exp(math.log(1.0) - 1.2078867 * jax.random.uniform(splits[2], (SECTIONS,), jnp.float32) ** steps_of(splits[2], (SECTIONS,), ((0, 2),), -0.2, 0.2)), 0.29882812, 1.0).astype(jnp.bfloat16),
        "spatial_kernel": normal_values(splits[3], (SECTIONS, 9, C, C), (12 * C) ** -0.5, 0.15625, ((0, 2),)),
        "temporal_kernel": normal_values(splits[4], (SECTIONS, 3, C, C), (12 * C) ** -0.5, 0.15625, ((0, 2),)),
        "output_weight": normal_values(splits[5], (SECTIONS, C, C), C ** -0.5, 0.5, ((0, 2),)),
    }


def denoise(previous, noise_part, noise_scale, spatial, temporal, out_weight):
    noisy = previous.astype(jnp.float32) + noise_scale * noise_part.astype(jnp.float32)
    normalized = (noisy * jax.lax.rsqrt(lax.optimization_barrier(jnp.mean(noisy * noisy, axis=-1, keepdims=True)) + 1e-05)).astype(jnp.bfloat16)
    bordered = jnp.pad(normalized, ((0, 0), (1, 1), (1, 1), (1, 1), (0, 0)))
    num_videos, num_frames, num_rows, num_cols, channels = previous.shape
    accumulated = jnp.zeros((num_videos * num_frames * num_rows * num_cols, channels), jnp.float32)
    for tap_index in range(9):
        row_offset = tap_index // 3
        col_offset = tap_index % 3
        shifted_view = bordered[:, 1:1 + num_frames, row_offset:row_offset + num_rows, col_offset:col_offset + num_cols, :]
        accumulated = accumulated + jnp.dot(shifted_view.reshape(-1, channels), spatial[tap_index], preferred_element_type=jnp.float32)
    for tap_index in range(3):
        shifted_view = bordered[:, tap_index:tap_index + num_frames, 1:1 + num_rows, 1:1 + num_cols, :]
        accumulated = accumulated + jnp.dot(shifted_view.reshape(-1, channels), temporal[tap_index], preferred_element_type=jnp.float32)
    activated = jax.nn.silu(accumulated).astype(jnp.bfloat16)
    estimate = jnp.dot(activated, out_weight, preferred_element_type=jnp.float32).reshape(previous.shape)
    return (noisy - noise_scale * estimate).astype(jnp.bfloat16)

def reference(base_frames, section_noise, noise_levels, spatial_kernel, temporal_kernel, output_weight):
    incoming = base_frames
    results = []
    for section_number in range(SECTIONS):
        level = noise_levels[section_number].astype(jnp.float32)
        produced = denoise(incoming, section_noise[section_number], level, spatial_kernel[section_number], temporal_kernel[section_number], output_weight[section_number])
        results.append(produced)
        incoming = produced
    return jnp.stack(results)
```

```python
import functools

import jax
import jax.numpy as jnp
from jax import lax
from jax.experimental import pallas as pl
from jax.experimental.pallas import tpu as pltpu
from jax.sharding import PartitionSpec as P

MESH = pl.DeviceIdType.MESH
SIDES = (("frames", 1), ("frames", -1), ("space", 1), ("space", -1))
CHUNK = 4


def kernel(
    videos, frames, rows, cols, channels,
    level_ref, base_hbm, noise_hbm, spatial_hbm, temporal_hbm, output_hbm, out_hbm,
    noise, prior, result, weights, noisy_ref, middle, before, after, edge_out, edge_in,
    noise_sem, base_sem, weight_sem, store_sem, chain_send, chain_recv, edge_send, edge_recv,
):
    place = {axis: lax.axis_index(axis) for axis in ("section", "frames", "space")}
    count = {axis: lax.axis_size(axis) for axis in place}

    def has(axis, step):
        return place[axis] < count[axis] - 1 if step > 0 else place[axis] > 0

    def peer(axis, step):
        return {axis: lax.rem(place[axis] + step + count[axis], count[axis])}

    first = place["section"] == 0
    onward = has("section", 1)

    def load_noise(v):
        return pltpu.make_async_copy(noise_hbm.at[v], noise.at[v], noise_sem.at[v])

    def load_base(v):
        return pltpu.make_async_copy(base_hbm.at[v], prior.at[v], base_sem.at[v])

    def store(v):
        return pltpu.make_async_copy(result.at[v], out_hbm.at[v], store_sem.at[v])

    def pass_on(v):
        return pltpu.make_async_remote_copy(
            src_ref=result.at[v], dst_ref=prior.at[v],
            send_sem=chain_send.at[v], recv_sem=chain_recv.at[v],
            device_id=peer("section", 1), device_id_type=MESH,
        )

    def edge(d, v):
        return pltpu.make_async_remote_copy(
            src_ref=edge_out.at[d, v], dst_ref=edge_in.at[d, v],
            send_sem=edge_send.at[d, v], recv_sem=edge_recv.at[d, v],
            device_id=peer(*SIDES[d]), device_id_type=MESH,
        )

    weight_loads = [
        pltpu.make_async_copy(spatial_hbm, weights.at[pl.ds(0, 9)], weight_sem.at[0]),
        pltpu.make_async_copy(temporal_hbm, weights.at[pl.ds(9, 3)], weight_sem.at[1]),
        pltpu.make_async_copy(output_hbm, weights.at[pl.ds(12, 1)], weight_sem.at[2]),
    ]

    neighbours = SIDES + (("section", 1), ("section", -1))
    barrier = pltpu.get_barrier_semaphore()
    for axis, step in neighbours:
        @pl.when(has(axis, step))
        def _():
            pl.semaphore_signal(barrier, inc=1, device_id=peer(axis, step), device_id_type=MESH)

    @pl.loop(0, videos)
    def _(v):
        load_noise(v).start()

        @pl.when(first)
        def _():
            load_base(v).start()

    for copy in weight_loads:
        copy.start()

    for d, (axis, step) in enumerate(SIDES):
        @pl.when(jnp.logical_not(has(axis, -step)))
        def _():
            edge_in[d] = jnp.zeros(edge_in.shape[1:], edge_in.dtype)

    pl.semaphore_wait(barrier, sum(has(*side).astype(jnp.int32) for side in neighbours))

    level = level_ref[...].astype(jnp.float32)

    def spread(v, x, at, size):
        lines = x.shape[0] * x.shape[1]
        flat = x.reshape(lines, cols, channels)
        column = lax.broadcasted_iota(jnp.int32, flat.shape, 1)
        left = jnp.where(column == 0, 0.0, pltpu.roll(flat, 1, 1))
        right = jnp.where(column == cols - 1, 0.0, pltpu.roll(flat, cols - 1, 1))
        middle[v, 1 : 1 + frames, at : at + size] = x
        before[v, :, at : at + size] = left.reshape(x.shape)
        after[v, :, at : at + size] = right.reshape(x.shape)

    def prepare(v):
        load_noise(v).wait()

        @pl.when(first)
        def _():
            load_base(v).wait()

        @pl.when(jnp.logical_not(first))
        def _():
            pass_on(v).wait_recv()

        noisy = prior[v].astype(jnp.float32) + level * noise[v].astype(jnp.float32)
        noisy_ref[v] = noisy
        power = jnp.mean(noisy * noisy, axis=-1, keepdims=True)
        normalized = (noisy * lax.rsqrt(power + 1e-05)).astype(jnp.bfloat16)
        x = normalized.astype(jnp.float32).reshape(frames, rows, cols, channels)
        edge_out[0, v] = normalized[frames - 1]
        edge_out[1, v] = normalized[0]
        edge_out[2, v] = x[:, rows - 1].reshape(frames * cols, channels).astype(jnp.bfloat16)
        edge_out[3, v] = x[:, 0].reshape(frames * cols, channels).astype(jnp.bfloat16)
        for d, side in enumerate(SIDES):
            @pl.when(has(*side))
            def _():
                edge(d, v).start()
        spread(v, x, 1, rows)

    def convolve(v):
        for d, (axis, step) in enumerate(SIDES):
            @pl.when(has(axis, -step))
            def _():
                edge(d, v).wait_recv()
        middle[v, 0, 1 : 1 + rows] = edge_in[0, v].astype(jnp.float32).reshape(rows, cols, channels)
        middle[v, frames + 1, 1 : 1 + rows] = (
            edge_in[1, v].astype(jnp.float32).reshape(rows, cols, channels)
        )
        for d, at in ((2, 0), (3, rows + 1)):
            spread(v, edge_in[d, v].astype(jnp.float32).reshape(frames, 1, cols, channels), at, 1)
        kernel_matrix = weights[0:12].reshape(12 * channels, channels)
        for f in range(0, frames, CHUNK):
            taps = []
            for a in range(3):
                for ref, skip in ((before, 0), (middle, 1), (after, 0)):
                    taps.append(ref[v, f + skip : f + skip + CHUNK, a : a + rows])
            for t in range(3):
                taps.append(middle[v, f + t : f + t + CHUNK, 1 : 1 + rows])
            taps = [tap.reshape(-1, channels).astype(jnp.bfloat16) for tap in taps]
            pre = jnp.dot(
                jnp.concatenate(taps, axis=-1), kernel_matrix, preferred_element_type=jnp.float32
            )
            activated = (pre / (1.0 + jnp.exp(-pre))).astype(jnp.bfloat16)
            estimate = jnp.dot(activated, weights[12], preferred_element_type=jnp.float32)
            held = noisy_ref[v, f : f + CHUNK]
            result[v, f : f + CHUNK] = (held - level * estimate.reshape(held.shape)).astype(
                jnp.bfloat16
            )

        @pl.when(onward)
        def _():
            pass_on(v).start()

        store(v).start()

    @pl.loop(0, videos + 1)
    def _(i):
        @pl.when(i < videos)
        def _():
            prepare(i)

        @pl.when(i == 1)
        def _():
            for copy in weight_loads:
                copy.wait()

        @pl.when(i > 0)
        def _():
            convolve(i - 1)

    @pl.loop(0, videos)
    def _(v):
        store(v).wait()

        @pl.when(onward)
        def _():
            pass_on(v).wait_send()

        for d, side in enumerate(SIDES):
            @pl.when(has(*side))
            def _():
                edge(d, v).wait_send()


def on_device(
    base_frames, section_noise, noise_levels, spatial_kernel, temporal_kernel, output_weight
):
    videos, frames, rows, cols, channels = base_frames.shape
    flat = (videos, frames, rows * cols, channels)
    wide = (videos, frames, rows + 2, cols, channels)
    edges = (len(SIDES), videos, frames * cols, channels)
    assert frames == rows and frames % CHUNK == 0
    result = pl.pallas_call(
        functools.partial(kernel, videos, frames, rows, cols, channels),
        out_shape=jax.ShapeDtypeStruct(flat, jnp.bfloat16),
        in_specs=[pl.BlockSpec(memory_space=pltpu.VMEM)] + [pl.BlockSpec(memory_space=pl.ANY)] * 5,
        out_specs=pl.BlockSpec(memory_space=pl.ANY),
        scratch_shapes=[
            pltpu.VMEM(flat, jnp.bfloat16),
            pltpu.VMEM(flat, jnp.bfloat16),
            pltpu.VMEM(flat, jnp.bfloat16),
            pltpu.VMEM((13, channels, channels), jnp.bfloat16),
            pltpu.VMEM(flat, jnp.float32),
            pltpu.VMEM((videos, frames + 2, rows + 2, cols, channels), jnp.float32),
            pltpu.VMEM(wide, jnp.float32),
            pltpu.VMEM(wide, jnp.float32),
            pltpu.VMEM(edges, jnp.bfloat16),
            pltpu.VMEM(edges, jnp.bfloat16),
            pltpu.SemaphoreType.DMA((videos,)),
            pltpu.SemaphoreType.DMA((videos,)),
            pltpu.SemaphoreType.DMA((3,)),
            pltpu.SemaphoreType.DMA((videos,)),
            pltpu.SemaphoreType.DMA((videos,)),
            pltpu.SemaphoreType.DMA((videos,)),
            pltpu.SemaphoreType.DMA((len(SIDES), videos)),
            pltpu.SemaphoreType.DMA((len(SIDES), videos)),
        ],
        compiler_params=pltpu.CompilerParams(
            collective_id=0, has_side_effects=True, vmem_limit_bytes=40 * 2**20
        ),
    )(
        noise_levels.reshape(1, 1),
        base_frames.reshape(flat),
        section_noise.reshape(flat),
        spatial_kernel[0],
        temporal_kernel[0],
        output_weight,
    )
    return result.reshape((1,) + base_frames.shape)


def solution(mesh):
    return jax.shard_map(
        on_device,
        mesh=mesh,
        in_specs=(
            P(None, "frames", "space", None, None),
            P("section", None, "frames", "space", None, None),
            P("section"),
            P("section", None, None, None),
            P("section", None, None, None),
            P("section", None, None),
        ),
        out_specs=P("section", None, "frames", "space", None, None),
        check_vma=False,
    )
```

```python
import functools

import jax
import jax.numpy as jnp
from jax import lax
from jax.experimental import pallas as pl
from jax.experimental.pallas import tpu as pltpu
from jax.sharding import PartitionSpec as P

MESH = pl.DeviceIdType.MESH
SIDES = (("frames", 1), ("frames", -1), ("space", 1), ("space", -1))
CHUNK = 4


def kernel(
    videos, ahead, frames, rows, cols, channels,
    level_ref, base_hbm, noise_hbm, spatial_hbm, temporal_hbm, output_hbm, out_hbm,
    noise, prior, result, weights, levels, level_out, level_in,
    noisy_ref, middle, before, after, edge_out, edge_in,
    noise_sem, base_sem, weight_sem, store_sem, chain_send, chain_recv, edge_send, edge_recv,
    lend_send, lend_recv,
):
    place = {axis: lax.axis_index(axis) for axis in ("section", "frames", "space")}
    count = {axis: lax.axis_size(axis) for axis in place}

    def has(axis, step):
        return place[axis] < count[axis] - 1 if step > 0 else place[axis] > 0

    def peer(axis, step):
        return {axis: lax.rem(place[axis] + step + count[axis], count[axis])}

    first = place["section"] == 0
    later = jnp.logical_not(first)
    onward = has("section", 1)
    items = videos + ahead
    lag = ahead + 1

    def special(v):
        return jnp.logical_and(v >= videos - lag, v < videos - 1) if ahead else False

    def active(j):
        if not ahead:
            return j < videos
        usual = jnp.logical_and(j < videos, jnp.logical_not(special(j)))
        return jnp.logical_or(usual, jnp.logical_and(first, j < items))

    def load_noise(v):
        return pltpu.make_async_copy(noise_hbm.at[v], noise.at[v], noise_sem.at[v])

    def load_base(v):
        return pltpu.make_async_copy(base_hbm.at[v], prior.at[v], base_sem.at[v])

    def store(v):
        return pltpu.make_async_copy(result.at[v], out_hbm.at[v], store_sem.at[v])

    def pass_on(v):
        return pltpu.make_async_remote_copy(
            src_ref=result.at[v], dst_ref=prior.at[v],
            send_sem=chain_send.at[v], recv_sem=chain_recv.at[v],
            device_id=peer("section", 1), device_id_type=MESH,
        )

    def finish(j):
        return pltpu.make_async_remote_copy(
            src_ref=result.at[j], dst_ref=out_hbm.at[j - lag],
            send_sem=chain_send.at[j], recv_sem=chain_recv.at[j],
            device_id=peer("section", 1), device_id_type=MESH,
        )

    def edge(d, v):
        return pltpu.make_async_remote_copy(
            src_ref=edge_out.at[d, v], dst_ref=edge_in.at[d, v],
            send_sem=edge_send.at[d, v], recv_sem=edge_recv.at[d, v],
            device_id=peer(*SIDES[d]), device_id_type=MESH,
        )

    parts = ((spatial_hbm, 0, 9), (temporal_hbm, 9, 3), (output_hbm, 12, 1))
    weight_loads = [
        pltpu.make_async_copy(source, weights.at[0, pl.ds(at, size)], weight_sem.at[n])
        for n, (source, at, size) in enumerate(parts)
    ]
    loans = []
    if ahead:
        pairs = [(level_out, level_in)]
        pairs += [(source, weights.at[1, pl.ds(at, size)]) for source, at, size in parts]
        for v in range(videos - lag, videos - 1):
            pairs.append((noise_hbm.at[v], noise.at[v + lag]))
        loans = [
            pltpu.make_async_remote_copy(
                src_ref=source, dst_ref=target, send_sem=lend_send.at[n], recv_sem=lend_recv.at[n],
                device_id=peer("section", -1), device_id_type=MESH,
            )
            for n, (source, target) in enumerate(pairs)
        ]

    def passes(v):
        if not ahead:
            return onward
        return jnp.logical_and(onward, jnp.logical_and(v < videos, jnp.logical_not(special(v))))

    neighbours = SIDES + (("section", 1), ("section", -1))
    barrier = pltpu.get_barrier_semaphore()
    for axis, step in neighbours:
        @pl.when(has(axis, step))
        def _():
            pl.semaphore_signal(barrier, inc=1, device_id=peer(axis, step), device_id_type=MESH)

    @pl.loop(0, videos)
    def _(v):
        @pl.when(active(v))
        def _():
            load_noise(v).start()

        @pl.when(first)
        def _():
            load_base(v).start()

    for copy in weight_loads:
        copy.start()

    for d, (axis, step) in enumerate(SIDES):
        @pl.when(jnp.logical_not(has(axis, -step)))
        def _():
            edge_in[d] = jnp.zeros(edge_in.shape[1:], edge_in.dtype)

    levels[0] = jnp.broadcast_to(level_ref[...].astype(jnp.float32), levels.shape[1:])
    level_out[...] = jnp.broadcast_to(level_ref[...], level_out.shape)

    def spread(v, x, at, size):
        lines = x.shape[0] * x.shape[1]
        flat = x.reshape(lines, cols, channels)
        column = lax.broadcasted_iota(jnp.int32, flat.shape, 1)
        left = jnp.where(column == 0, 0.0, pltpu.roll(flat, 1, 1))
        right = jnp.where(column == cols - 1, 0.0, pltpu.roll(flat, cols - 1, 1))
        middle[v, 1 : 1 + frames, at : at + size] = x
        before[v, :, at : at + size] = left.reshape(x.shape)
        after[v, :, at : at + size] = right.reshape(x.shape)

    def normalise(v, number):
        noisy = prior[v].astype(jnp.float32) + levels[number][0:1] * noise[v].astype(jnp.float32)
        noisy_ref[v] = noisy
        power = jnp.mean(noisy * noisy, axis=-1, keepdims=True)
        normalized = (noisy * lax.rsqrt(power + 1e-05)).astype(jnp.bfloat16)
        x = normalized.astype(jnp.float32).reshape(frames, rows, cols, channels)
        edge_out[0, v] = normalized[frames - 1]
        edge_out[1, v] = normalized[0]
        edge_out[2, v] = x[:, rows - 1].reshape(frames * cols, channels).astype(jnp.bfloat16)
        edge_out[3, v] = x[:, 0].reshape(frames * cols, channels).astype(jnp.bfloat16)
        spread(v, x, 1, rows)

    def send_edges(v):
        for d, side in enumerate(SIDES):
            @pl.when(has(*side))
            def _():
                edge(d, v).start()

    def prepare(i):
        @pl.when(i < videos)
        def _():
            load_noise(i).wait()

            @pl.when(first)
            def _():
                load_base(i).wait()

            @pl.when(later)
            def _():
                pass_on(i).wait_recv()

        if ahead:
            @pl.when(i == videos)
            def _():
                for copy in loans:
                    copy.wait_recv()
                levels[1] = level_in[0:8].astype(jnp.float32)

            @pl.when(i >= videos)
            def _():
                prior[i] = result[i - lag]

        normalise(i, (i >= videos).astype(jnp.int32) if ahead else 0)

    def convolve(v):
        for d, (axis, step) in enumerate(SIDES):
            @pl.when(has(axis, -step))
            def _():
                edge(d, v).wait_recv()
        number = (v >= videos).astype(jnp.int32) if ahead else 0
        middle[v, 0, 1 : 1 + rows] = edge_in[0, v].astype(jnp.float32).reshape(rows, cols, channels)
        middle[v, frames + 1, 1 : 1 + rows] = (
            edge_in[1, v].astype(jnp.float32).reshape(rows, cols, channels)
        )
        for d, at in ((2, 0), (3, rows + 1)):
            spread(v, edge_in[d, v].astype(jnp.float32).reshape(frames, 1, cols, channels), at, 1)
        kernel_matrix = weights[number, 0:12].reshape(12 * channels, channels)
        projection = weights[number, 12]
        level = levels[number][0:1]
        for f in range(0, frames, CHUNK):
            taps = []
            for a in range(3):
                for ref, skip in ((before, 0), (middle, 1), (after, 0)):
                    taps.append(ref[v, f + skip : f + skip + CHUNK, a : a + rows])
            for t in range(3):
                taps.append(middle[v, f + t : f + t + CHUNK, 1 : 1 + rows])
            taps = [tap.reshape(-1, channels).astype(jnp.bfloat16) for tap in taps]
            pre = jnp.dot(
                jnp.concatenate(taps, axis=-1), kernel_matrix, preferred_element_type=jnp.float32
            )
            activated = (pre / (1.0 + jnp.exp(-pre))).astype(jnp.bfloat16)
            estimate = jnp.dot(activated, projection, preferred_element_type=jnp.float32)
            held = noisy_ref[v, f : f + CHUNK]
            result[v, f : f + CHUNK] = (held - level * estimate.reshape(held.shape)).astype(
                jnp.bfloat16
            )

        @pl.when(passes(v))
        def _():
            pass_on(v).start()

        @pl.when(v < videos)
        def _():
            store(v).start()

        if ahead:
            @pl.when(v >= videos)
            def _():
                finish(v).start()

    @pl.when(first)
    def _():
        load_noise(0).wait()
        load_base(0).wait()
        normalise(0, 0)

    pl.semaphore_wait(barrier, sum(has(*side).astype(jnp.int32) for side in neighbours))

    @pl.when(first)
    def _():
        send_edges(0)

    if ahead:
        @pl.when(later)
        def _():
            for copy in loans:
                copy.start()

    @pl.loop(0, items + 1)
    def _(i):
        @pl.when(jnp.logical_and(active(i), jnp.logical_or(i > 0, later)))
        def _():
            prepare(i)
            send_edges(i)

        @pl.when(i == 1)
        def _():
            for copy in weight_loads:
                copy.wait()

        @pl.when(jnp.logical_and(i > 0, active(i - 1)))
        def _():
            convolve(i - 1)

    @pl.loop(0, items)
    def _(j):
        @pl.when(active(j))
        def _():
            @pl.when(j < videos)
            def _():
                store(j).wait()

            @pl.when(passes(j))
            def _():
                pass_on(j).wait_send()

            if ahead:
                @pl.when(j >= videos)
                def _():
                    finish(j).wait_send()

            for d, side in enumerate(SIDES):
                @pl.when(has(*side))
                def _():
                    edge(d, j).wait_send()

    if ahead:
        @pl.when(later)
        def _():
            for copy in loans:
                copy.wait_send()
            for j in range(videos, items):
                finish(j).wait_recv()


def on_device(
    base_frames, section_noise, noise_levels, spatial_kernel, temporal_kernel, output_weight
):
    videos, frames, rows, cols, channels = base_frames.shape
    ahead = 1 if lax.axis_size("section") == 2 and videos > 2 else 0
    items = videos + ahead
    flat = (frames, rows * cols, channels)
    wide = (items, frames, rows + 2, cols, channels)
    edges = (len(SIDES), items, frames * cols, channels)
    assert frames == rows and frames % CHUNK == 0
    result = pl.pallas_call(
        functools.partial(kernel, videos, ahead, frames, rows, cols, channels),
        out_shape=jax.ShapeDtypeStruct((videos,) + flat, jnp.bfloat16),
        in_specs=[pl.BlockSpec(memory_space=pltpu.VMEM)] + [pl.BlockSpec(memory_space=pl.ANY)] * 5,
        out_specs=pl.BlockSpec(memory_space=pl.ANY),
        scratch_shapes=[
            pltpu.VMEM((items,) + flat, jnp.bfloat16),
            pltpu.VMEM((items,) + flat, jnp.bfloat16),
            pltpu.VMEM((items,) + flat, jnp.bfloat16),
            pltpu.VMEM((1 + ahead, 13, channels, channels), jnp.bfloat16),
            pltpu.VMEM((1 + ahead, 8, channels), jnp.float32),
            pltpu.VMEM((16, channels), jnp.bfloat16),
            pltpu.VMEM((16, channels), jnp.bfloat16),
            pltpu.VMEM((items,) + flat, jnp.float32),
            pltpu.VMEM((items, frames + 2, rows + 2, cols, channels), jnp.float32),
            pltpu.VMEM(wide, jnp.float32),
            pltpu.VMEM(wide, jnp.float32),
            pltpu.VMEM(edges, jnp.bfloat16),
            pltpu.VMEM(edges, jnp.bfloat16),
            pltpu.SemaphoreType.DMA((videos,)),
            pltpu.SemaphoreType.DMA((videos,)),
            pltpu.SemaphoreType.DMA((3,)),
            pltpu.SemaphoreType.DMA((videos,)),
            pltpu.SemaphoreType.DMA((items,)),
            pltpu.SemaphoreType.DMA((items,)),
            pltpu.SemaphoreType.DMA((len(SIDES), items)),
            pltpu.SemaphoreType.DMA((len(SIDES), items)),
            pltpu.SemaphoreType.DMA((4 + videos,)),
            pltpu.SemaphoreType.DMA((4 + videos,)),
        ],
        compiler_params=pltpu.CompilerParams(
            collective_id=0, has_side_effects=True, vmem_limit_bytes=62 * 2**20
        ),
    )(
        noise_levels.reshape(1, 1),
        base_frames.reshape((videos,) + flat),
        section_noise.reshape((videos,) + flat),
        spatial_kernel[0],
        temporal_kernel[0],
        output_weight,
    )
    return result.reshape((1,) + base_frames.shape)


def solution(mesh):
    return jax.shard_map(
        on_device,
        mesh=mesh,
        in_specs=(
            P(None, "frames", "space", None, None),
            P("section", None, "frames", "space", None, None),
            P("section"),
            P("section", None, None, None),
            P("section", None, None, None),
            P("section", None, None),
        ),
        out_specs=P("section", None, "frames", "space", None, None),
        check_vma=False,
    )
```

```python
import functools

import jax
import jax.numpy as jnp
from jax import lax
from jax.experimental import pallas as pl
from jax.experimental.pallas import tpu as pltpu
from jax.sharding import PartitionSpec as P

MESH = pl.DeviceIdType.MESH
SIDES = (("frames", 1), ("frames", -1), ("space", 1), ("space", -1))
CHUNK = 4


def kernel(
    videos, ahead, frames, rows, cols, channels,
    level_ref, base_hbm, noise_hbm, spatial_hbm, temporal_hbm, output_hbm, out_hbm,
    noise, prior, result, weights, packed, levels, level_out, level_in,
    noisy_ref, middle, edge_out, edge_in,
    noise_sem, base_sem, weight_sem, store_sem, chain_send, chain_recv, edge_send, edge_recv,
    lend_send, lend_recv,
):
    place = {axis: lax.axis_index(axis) for axis in ("section", "frames", "space")}
    count = {axis: lax.axis_size(axis) for axis in place}

    def has(axis, step):
        return place[axis] < count[axis] - 1 if step > 0 else place[axis] > 0

    def peer(axis, step):
        return {axis: lax.rem(place[axis] + step + count[axis], count[axis])}

    first = place["section"] == 0
    later = jnp.logical_not(first)
    onward = has("section", 1)
    items = videos + ahead
    lag = ahead + 1

    def special(v):
        return jnp.logical_and(v >= videos - lag, v < videos - 1) if ahead else False

    def active(j):
        if not ahead:
            return j < videos
        usual = jnp.logical_and(j < videos, jnp.logical_not(special(j)))
        return jnp.logical_or(usual, jnp.logical_and(first, j < items))

    def load_noise(v):
        return pltpu.make_async_copy(noise_hbm.at[v], noise.at[v], noise_sem.at[v])

    def load_base(v):
        return pltpu.make_async_copy(base_hbm.at[v], prior.at[v], base_sem.at[v])

    def store(v):
        return pltpu.make_async_copy(result.at[v], out_hbm.at[v], store_sem.at[v])

    def pass_on(v):
        return pltpu.make_async_remote_copy(
            src_ref=result.at[v], dst_ref=prior.at[v],
            send_sem=chain_send.at[v], recv_sem=chain_recv.at[v],
            device_id=peer("section", 1), device_id_type=MESH,
        )

    def finish(j):
        return pltpu.make_async_remote_copy(
            src_ref=result.at[j], dst_ref=out_hbm.at[j - lag],
            send_sem=chain_send.at[j], recv_sem=chain_recv.at[j],
            device_id=peer("section", 1), device_id_type=MESH,
        )

    def edge(d, v):
        return pltpu.make_async_remote_copy(
            src_ref=edge_out.at[d, v], dst_ref=edge_in.at[d, v],
            send_sem=edge_send.at[d, v], recv_sem=edge_recv.at[d, v],
            device_id=peer(*SIDES[d]), device_id_type=MESH,
        )

    parts = ((spatial_hbm, 0, 9), (temporal_hbm, 9, 3), (output_hbm, 12, 1))
    weight_loads = [
        pltpu.make_async_copy(source, weights.at[0, pl.ds(at, size)], weight_sem.at[n])
        for n, (source, at, size) in enumerate(parts)
    ]
    loans = []
    if ahead:
        pairs = [(level_out, level_in)]
        pairs += [(source, weights.at[1, pl.ds(at, size)]) for source, at, size in parts]
        for v in range(videos - lag, videos - 1):
            pairs.append((noise_hbm.at[v], noise.at[v + lag]))
        loans = [
            pltpu.make_async_remote_copy(
                src_ref=source, dst_ref=target, send_sem=lend_send.at[n], recv_sem=lend_recv.at[n],
                device_id=peer("section", -1), device_id_type=MESH,
            )
            for n, (source, target) in enumerate(pairs)
        ]

    def passes(v):
        if not ahead:
            return onward
        return jnp.logical_and(onward, jnp.logical_and(v < videos, jnp.logical_not(special(v))))

    neighbours = SIDES + (("section", 1), ("section", -1))
    barrier = pltpu.get_barrier_semaphore()
    for axis, step in neighbours:
        @pl.when(has(axis, step))
        def _():
            pl.semaphore_signal(barrier, inc=1, device_id=peer(axis, step), device_id_type=MESH)

    @pl.loop(0, videos)
    def _(v):
        @pl.when(active(v))
        def _():
            load_noise(v).start()

        @pl.when(first)
        def _():
            load_base(v).start()

    for copy in weight_loads:
        copy.start()

    for d, (axis, step) in enumerate(SIDES):
        @pl.when(jnp.logical_not(has(axis, -step)))
        def _():
            edge_in[d] = jnp.zeros(edge_in.shape[1:], edge_in.dtype)

    levels[0] = jnp.broadcast_to(level_ref[...].astype(jnp.float32), levels.shape[1:])
    level_out[...] = jnp.broadcast_to(level_ref[...], level_out.shape)

    def pack(number):
        packed[number] = jnp.zeros(packed.shape[1:], packed.dtype)
        for a in range(3):
            line = pl.ds(a * channels, channels)
            packed[number, 0, line, :channels] = weights[number, 3 * a + 1]
            packed[number, 0, line, channels:] = weights[number, 3 * a + 2]
            packed[number, 1, line, :channels] = weights[number, 3 * a]
        packed[number, 0, 3 * channels :, :channels] = weights[number, 9]
        packed[number, 1, channels : 2 * channels, channels:] = weights[number, 10]
        packed[number, 1, 3 * channels :, channels:] = weights[number, 11]

    def normalise(v, number):
        noisy = prior[v].astype(jnp.float32) + levels[number][0:1] * noise[v].astype(jnp.float32)
        noisy_ref[v] = noisy
        power = jnp.mean(noisy * noisy, axis=-1, keepdims=True)
        normalized = (noisy * lax.rsqrt(power + 1e-05)).astype(jnp.bfloat16)
        x = normalized.astype(jnp.float32).reshape(frames, rows, cols, channels)
        edge_out[0, v] = normalized[frames - 1]
        edge_out[1, v] = normalized[0]
        edge_out[2, v] = x[:, rows - 1].reshape(frames * cols, channels).astype(jnp.bfloat16)
        edge_out[3, v] = x[:, 0].reshape(frames * cols, channels).astype(jnp.bfloat16)
        middle[v, 1 : 1 + frames, 1 : 1 + rows] = x

    def send_edges(v):
        for d, side in enumerate(SIDES):
            @pl.when(has(*side))
            def _():
                edge(d, v).start()

    def prepare(i):
        @pl.when(i < videos)
        def _():
            load_noise(i).wait()

            @pl.when(first)
            def _():
                load_base(i).wait()

            @pl.when(later)
            def _():
                pass_on(i).wait_recv()

        if ahead:
            @pl.when(i == videos)
            def _():
                for copy in loans:
                    copy.wait_recv()
                levels[1] = level_in[0:8].astype(jnp.float32)
                pack(1)

            @pl.when(i >= videos)
            def _():
                prior[i] = result[i - lag]

        normalise(i, (i >= videos).astype(jnp.int32) if ahead else 0)

    def convolve(v):
        for d, (axis, step) in enumerate(SIDES):
            @pl.when(has(axis, -step))
            def _():
                edge(d, v).wait_recv()
        number = (v >= videos).astype(jnp.int32) if ahead else 0
        middle[v, 0, 1 : 1 + rows] = edge_in[0, v].astype(jnp.float32).reshape(rows, cols, channels)
        middle[v, frames + 1, 1 : 1 + rows] = (
            edge_in[1, v].astype(jnp.float32).reshape(rows, cols, channels)
        )
        for d, at in ((2, 0), (3, rows + 1)):
            middle[v, 1 : 1 + frames, at] = (
                edge_in[d, v].astype(jnp.float32).reshape(frames, cols, channels)
            )
        projection = weights[number, 12]
        level = levels[number][0:1]
        lines = CHUNK * rows
        column = lax.broadcasted_iota(jnp.int32, (lines, cols, channels), 1)
        for f in range(0, frames, CHUNK):
            views = [middle[v, f + 1 : f + 1 + CHUNK, a : a + rows] for a in range(3)]
            views += [middle[v, f + t : f + t + CHUNK, 1 : 1 + rows] for t in (0, 2)]
            views = [view.reshape(-1, channels).astype(jnp.bfloat16) for view in views]
            sums = [
                jnp.dot(
                    jnp.concatenate(views[:3] + [views[3 + n]], axis=-1), packed[number, n],
                    preferred_element_type=jnp.float32,
                )
                for n in range(2)
            ]
            ahead_part = sums[0][:, channels:].reshape(lines, cols, channels)
            behind_part = sums[1][:, :channels].reshape(lines, cols, channels)
            shifted = jnp.where(column == cols - 1, 0.0, pltpu.roll(ahead_part, cols - 1, 1))
            shifted = shifted + jnp.where(column == 0, 0.0, pltpu.roll(behind_part, 1, 1))
            pre = sums[0][:, :channels] + sums[1][:, channels:] + shifted.reshape(-1, channels)
            activated = (pre / (1.0 + jnp.exp(-pre))).astype(jnp.bfloat16)
            estimate = jnp.dot(activated, projection, preferred_element_type=jnp.float32)
            held = noisy_ref[v, f : f + CHUNK]
            result[v, f : f + CHUNK] = (held - level * estimate.reshape(held.shape)).astype(
                jnp.bfloat16
            )

        @pl.when(passes(v))
        def _():
            pass_on(v).start()

        @pl.when(v < videos)
        def _():
            store(v).start()

        if ahead:
            @pl.when(v >= videos)
            def _():
                finish(v).start()

    @pl.when(first)
    def _():
        load_noise(0).wait()
        load_base(0).wait()
        normalise(0, 0)

    pl.semaphore_wait(barrier, sum(has(*side).astype(jnp.int32) for side in neighbours))

    @pl.when(first)
    def _():
        send_edges(0)

    if ahead:
        @pl.when(later)
        def _():
            for copy in loans:
                copy.start()

    @pl.loop(0, items + 1)
    def _(i):
        @pl.when(jnp.logical_and(active(i), jnp.logical_or(i > 0, later)))
        def _():
            prepare(i)
            send_edges(i)

        @pl.when(i == 1)
        def _():
            for copy in weight_loads:
                copy.wait()
            pack(0)

        @pl.when(jnp.logical_and(i > 0, active(i - 1)))
        def _():
            convolve(i - 1)

    @pl.loop(0, items)
    def _(j):
        @pl.when(active(j))
        def _():
            @pl.when(j < videos)
            def _():
                store(j).wait()

            @pl.when(passes(j))
            def _():
                pass_on(j).wait_send()

            if ahead:
                @pl.when(j >= videos)
                def _():
                    finish(j).wait_send()

            for d, side in enumerate(SIDES):
                @pl.when(has(*side))
                def _():
                    edge(d, j).wait_send()

    if ahead:
        @pl.when(later)
        def _():
            for copy in loans:
                copy.wait_send()
            for j in range(videos, items):
                finish(j).wait_recv()


def on_device(
    base_frames, section_noise, noise_levels, spatial_kernel, temporal_kernel, output_weight
):
    videos, frames, rows, cols, channels = base_frames.shape
    ahead = 1 if lax.axis_size("section") == 2 and videos > 2 else 0
    items = videos + ahead
    flat = (frames, rows * cols, channels)
    edges = (len(SIDES), items, frames * cols, channels)
    assert frames == rows and frames % CHUNK == 0
    result = pl.pallas_call(
        functools.partial(kernel, videos, ahead, frames, rows, cols, channels),
        out_shape=jax.ShapeDtypeStruct((videos,) + flat, jnp.bfloat16),
        in_specs=[pl.BlockSpec(memory_space=pltpu.VMEM)] + [pl.BlockSpec(memory_space=pltpu.HBM)] * 5,
        out_specs=pl.BlockSpec(memory_space=pl.ANY),
        scratch_shapes=[
            pltpu.VMEM((items,) + flat, jnp.bfloat16),
            pltpu.VMEM((items,) + flat, jnp.bfloat16),
            pltpu.VMEM((items,) + flat, jnp.bfloat16),
            pltpu.VMEM((1 + ahead, 13, channels, channels), jnp.bfloat16),
            pltpu.VMEM((1 + ahead, 2, 4 * channels, 2 * channels), jnp.bfloat16),
            pltpu.VMEM((1 + ahead, 8, channels), jnp.float32),
            pltpu.VMEM((16, channels), jnp.bfloat16),
            pltpu.VMEM((16, channels), jnp.bfloat16),
            pltpu.VMEM((items,) + flat, jnp.float32),
            pltpu.VMEM((items, frames + 2, rows + 2, cols, channels), jnp.float32),
            pltpu.VMEM(edges, jnp.bfloat16),
            pltpu.VMEM(edges, jnp.bfloat16),
            pltpu.SemaphoreType.DMA((videos,)),
            pltpu.SemaphoreType.DMA((videos,)),
            pltpu.SemaphoreType.DMA((3,)),
            pltpu.SemaphoreType.DMA((videos,)),
            pltpu.SemaphoreType.DMA((items,)),
            pltpu.SemaphoreType.DMA((items,)),
            pltpu.SemaphoreType.DMA((len(SIDES), items)),
            pltpu.SemaphoreType.DMA((len(SIDES), items)),
            pltpu.SemaphoreType.DMA((4 + videos,)),
            pltpu.SemaphoreType.DMA((4 + videos,)),
        ],
        compiler_params=pltpu.CompilerParams(
            collective_id=0, has_side_effects=True, vmem_limit_bytes=58 * 2**20
        ),
    )(
        noise_levels.reshape(1, 1),
        base_frames.reshape((videos,) + flat),
        section_noise.reshape((videos,) + flat),
        spatial_kernel[0],
        temporal_kernel[0],
        output_weight,
    )
    return result.reshape((1,) + base_frames.shape)


def solution(mesh):
    return jax.shard_map(
        on_device,
        mesh=mesh,
        in_specs=(
            P(None, "frames", "space", None, None),
            P("section", None, "frames", "space", None, None),
            P("section"),
            P("section", None, None, None),
            P("section", None, None, None),
            P("section", None, None),
        ),
        out_specs=P("section", None, "frames", "space", None, None),
        check_vma=False,
    )
```

```python
import functools

import jax
import jax.numpy as jnp
from jax import lax
from jax.experimental import pallas as pl
from jax.experimental.pallas import tpu as pltpu
from jax.sharding import PartitionSpec as P

MESH = pl.DeviceIdType.MESH
SIDES = (("frames", 1), ("frames", -1), ("space", 1), ("space", -1))
CHUNK = 4


def kernel(
    videos, ahead, frames, rows, cols, channels,
    level_ref, base_hbm, noise_hbm, spatial_hbm, temporal_hbm, output_hbm, out_ref,
    noise, prior, result, weights, packed, levels, level_out, level_in,
    noisy_ref, middle, edge_out, edge_in,
    noise_sem, base_sem, weight_sem, chain_send, chain_recv, edge_send, edge_recv,
    lend_send, lend_recv,
):
    place = {axis: lax.axis_index(axis) for axis in ("section", "frames", "space")}
    count = {axis: lax.axis_size(axis) for axis in place}

    def has(axis, step):
        return place[axis] < count[axis] - 1 if step > 0 else place[axis] > 0

    def peer(axis, step):
        return {axis: lax.rem(place[axis] + step + count[axis], count[axis])}

    first = place["section"] == 0
    later = jnp.logical_not(first)
    onward = has("section", 1)
    items = videos + ahead
    lag = ahead + 1

    def special(v):
        return jnp.logical_and(v >= videos - lag, v < videos - 1) if ahead else False

    def active(j):
        if not ahead:
            return j < videos
        usual = jnp.logical_and(j < videos, jnp.logical_not(special(j)))
        return jnp.logical_or(usual, jnp.logical_and(first, j < items))

    def load_noise(v):
        return pltpu.make_async_copy(noise_hbm.at[v], noise.at[v], noise_sem.at[v])

    def load_base(v):
        return pltpu.make_async_copy(base_hbm.at[v], prior.at[v], base_sem.at[v])

    def pass_on(v):
        return pltpu.make_async_remote_copy(
            src_ref=result.at[v], dst_ref=prior.at[v],
            send_sem=chain_send.at[v], recv_sem=chain_recv.at[v],
            device_id=peer("section", 1), device_id_type=MESH,
        )

    def finish(j):
        return pltpu.make_async_remote_copy(
            src_ref=result.at[j], dst_ref=out_ref.at[j - lag],
            send_sem=chain_send.at[j], recv_sem=chain_recv.at[j],
            device_id=peer("section", 1), device_id_type=MESH,
        )

    def edge(d, v):
        return pltpu.make_async_remote_copy(
            src_ref=edge_out.at[d, v], dst_ref=edge_in.at[d, v],
            send_sem=edge_send.at[d, v], recv_sem=edge_recv.at[d, v],
            device_id=peer(*SIDES[d]), device_id_type=MESH,
        )

    parts = ((spatial_hbm, 0, 9), (temporal_hbm, 9, 3), (output_hbm, 12, 1))
    weight_loads = [
        pltpu.make_async_copy(source, weights.at[0, pl.ds(at, size)], weight_sem.at[n])
        for n, (source, at, size) in enumerate(parts)
    ]
    loans = []
    if ahead:
        pairs = [(level_out, level_in)]
        pairs += [(source, weights.at[1, pl.ds(at, size)]) for source, at, size in parts]
        for v in range(videos - lag, videos - 1):
            pairs.append((noise_hbm.at[v], noise.at[v + lag]))
        loans = [
            pltpu.make_async_remote_copy(
                src_ref=source, dst_ref=target, send_sem=lend_send.at[n], recv_sem=lend_recv.at[n],
                device_id=peer("section", -1), device_id_type=MESH,
            )
            for n, (source, target) in enumerate(pairs)
        ]

    def passes(v):
        if not ahead:
            return onward
        return jnp.logical_and(onward, jnp.logical_and(v < videos, jnp.logical_not(special(v))))

    def sends(v):
        return jnp.logical_or(passes(v), v >= videos)

    def before(v):
        return v - 1 - ahead * (v == videos - 1).astype(jnp.int32)

    neighbours = SIDES + (("section", 1), ("section", -1))
    barrier = pltpu.get_barrier_semaphore()
    for axis, step in neighbours:
        @pl.when(has(axis, step))
        def _():
            pl.semaphore_signal(barrier, inc=1, device_id=peer(axis, step), device_id_type=MESH)

    @pl.loop(0, videos)
    def _(v):
        @pl.when(active(v))
        def _():
            load_noise(v).start()

        @pl.when(first)
        def _():
            load_base(v).start()

    for copy in weight_loads:
        copy.start()

    for d, (axis, step) in enumerate(SIDES):
        @pl.when(jnp.logical_not(has(axis, -step)))
        def _():
            edge_in[d] = jnp.zeros(edge_in.shape[1:], edge_in.dtype)

    levels[0] = jnp.broadcast_to(level_ref[...].astype(jnp.float32), levels.shape[1:])
    level_out[...] = jnp.broadcast_to(level_ref[...], level_out.shape)

    def pack(number):
        packed[number] = jnp.zeros(packed.shape[1:], packed.dtype)
        for a in range(3):
            line = pl.ds(a * channels, channels)
            packed[number, 0, line, :channels] = weights[number, 3 * a + 1]
            packed[number, 0, line, channels:] = weights[number, 3 * a + 2]
            packed[number, 1, line, :channels] = weights[number, 3 * a]
        packed[number, 0, 3 * channels :, :channels] = weights[number, 9]
        packed[number, 1, channels : 2 * channels, channels:] = weights[number, 10]
        packed[number, 1, 3 * channels :, channels:] = weights[number, 11]

    def normalise(v, number):
        noisy = prior[v].astype(jnp.float32) + levels[number][0:1] * noise[v].astype(jnp.float32)
        noisy_ref[v] = noisy
        power = jnp.mean(noisy * noisy, axis=-1, keepdims=True)
        normalized = (noisy * lax.rsqrt(power + 1e-05)).astype(jnp.bfloat16)
        x = normalized.astype(jnp.float32).reshape(frames, rows, cols, channels)
        edge_out[0, v] = normalized[frames - 1]
        edge_out[1, v] = normalized[0]
        edge_out[2, v] = x[:, rows - 1].reshape(frames * cols, channels).astype(jnp.bfloat16)
        edge_out[3, v] = x[:, 0].reshape(frames * cols, channels).astype(jnp.bfloat16)
        middle[v, 1 : 1 + frames, 1 : 1 + rows] = x

    def send_edges(v):
        for d, side in enumerate(SIDES):
            @pl.when(has(*side))
            def _():
                edge(d, v).start()

    def prepare(i):
        @pl.when(i < videos)
        def _():
            load_noise(i).wait()

            @pl.when(first)
            def _():
                load_base(i).wait()

            @pl.when(later)
            def _():
                pass_on(i).wait_recv()

        if ahead:
            @pl.when(i == videos)
            def _():
                for copy in loans:
                    copy.wait_recv()
                levels[1] = level_in[0:8].astype(jnp.float32)
                pack(1)

            @pl.when(i >= videos)
            def _():
                prior[i] = result[i - lag]

        normalise(i, (i >= videos).astype(jnp.int32) if ahead else 0)

    def convolve(v):
        for d, (axis, step) in enumerate(SIDES):
            @pl.when(has(axis, -step))
            def _():
                edge(d, v).wait_recv()
        number = (v >= videos).astype(jnp.int32) if ahead else 0
        middle[v, 0, 1 : 1 + rows] = edge_in[0, v].astype(jnp.float32).reshape(rows, cols, channels)
        middle[v, frames + 1, 1 : 1 + rows] = (
            edge_in[1, v].astype(jnp.float32).reshape(rows, cols, channels)
        )
        for d, at in ((2, 0), (3, rows + 1)):
            middle[v, 1 : 1 + frames, at] = (
                edge_in[d, v].astype(jnp.float32).reshape(frames, cols, channels)
            )
        projection = weights[number, 12]
        level = levels[number][0:1]
        lines = CHUNK * rows
        column = lax.broadcasted_iota(jnp.int32, (lines, cols, channels), 1)
        for f in range(0, frames, CHUNK):
            views = [middle[v, f + 1 : f + 1 + CHUNK, a : a + rows] for a in range(3)]
            views += [middle[v, f + t : f + t + CHUNK, 1 : 1 + rows] for t in (0, 2)]
            views = [view.reshape(-1, channels).astype(jnp.bfloat16) for view in views]
            sums = [
                jnp.dot(
                    jnp.concatenate(views[:3] + [views[3 + n]], axis=-1), packed[number, n],
                    preferred_element_type=jnp.float32,
                )
                for n in range(2)
            ]
            ahead_part = sums[0][:, channels:].reshape(lines, cols, channels)
            behind_part = sums[1][:, :channels].reshape(lines, cols, channels)
            shifted = jnp.where(column == cols - 1, 0.0, pltpu.roll(ahead_part, cols - 1, 1))
            shifted = shifted + jnp.where(column == 0, 0.0, pltpu.roll(behind_part, 1, 1))
            pre = sums[0][:, :channels] + sums[1][:, channels:] + shifted.reshape(-1, channels)
            activated = (pre / (1.0 + jnp.exp(-pre))).astype(jnp.bfloat16)
            estimate = jnp.dot(activated, projection, preferred_element_type=jnp.float32)
            held = noisy_ref[v, f : f + CHUNK]
            result[v, f : f + CHUNK] = (held - level * estimate.reshape(held.shape)).astype(
                jnp.bfloat16
            )

        @pl.when(jnp.logical_and(v > 0, sends(v)))
        def _():
            pass_on(before(v)).wait_send()

        @pl.when(passes(v))
        def _():
            pass_on(v).start()

        if ahead:
            @pl.when(v >= videos)
            def _():
                finish(v).start()

        @pl.when(v < videos)
        def _():
            out_ref[v] = result[v]

    @pl.when(first)
    def _():
        load_noise(0).wait()
        load_base(0).wait()
        normalise(0, 0)

    pl.semaphore_wait(barrier, sum(has(*side).astype(jnp.int32) for side in neighbours))

    @pl.when(first)
    def _():
        send_edges(0)

    if ahead:
        @pl.when(later)
        def _():
            for copy in loans:
                copy.start()

    @pl.loop(0, items + 1)
    def _(i):
        @pl.when(jnp.logical_and(active(i), jnp.logical_or(i > 0, later)))
        def _():
            prepare(i)
            send_edges(i)

        @pl.when(i == 1)
        def _():
            for copy in weight_loads:
                copy.wait()
            pack(0)

        @pl.when(jnp.logical_and(i > 0, active(i - 1)))
        def _():
            convolve(i - 1)

    @pl.loop(0, items)
    def _(j):
        @pl.when(active(j))
        def _():
            for d, side in enumerate(SIDES):
                @pl.when(has(*side))
                def _():
                    edge(d, j).wait_send()

    @pl.when(onward)
    def _():
        if ahead:
            finish(items - 1).wait_send()
        else:
            pass_on(videos - 1).wait_send()

    if ahead:
        @pl.when(later)
        def _():
            for copy in loans:
                copy.wait_send()
            for j in range(videos, items):
                finish(j).wait_recv()


def on_device(
    base_frames, section_noise, noise_levels, spatial_kernel, temporal_kernel, output_weight
):
    videos, frames, rows, cols, channels = base_frames.shape
    ahead = 1 if lax.axis_size("section") == 2 and videos > 2 else 0
    items = videos + ahead
    flat = (frames, rows * cols, channels)
    edges = (len(SIDES), items, frames * cols, channels)
    assert frames == rows and frames % CHUNK == 0
    result = pl.pallas_call(
        functools.partial(kernel, videos, ahead, frames, rows, cols, channels),
        out_shape=pltpu.VMEM((videos,) + flat, jnp.bfloat16),
        in_specs=[pl.BlockSpec(memory_space=pltpu.VMEM)] + [pl.BlockSpec(memory_space=pltpu.HBM)] * 5,
        out_specs=pl.BlockSpec(memory_space=pltpu.VMEM),
        scratch_shapes=[
            pltpu.VMEM((items,) + flat, jnp.bfloat16),
            pltpu.VMEM((items,) + flat, jnp.bfloat16),
            pltpu.VMEM((items,) + flat, jnp.bfloat16),
            pltpu.VMEM((1 + ahead, 13, channels, channels), jnp.bfloat16),
            pltpu.VMEM((1 + ahead, 2, 4 * channels, 2 * channels), jnp.bfloat16),
            pltpu.VMEM((1 + ahead, 8, channels), jnp.float32),
            pltpu.VMEM((16, channels), jnp.bfloat16),
            pltpu.VMEM((16, channels), jnp.bfloat16),
            pltpu.VMEM((items,) + flat, jnp.float32),
            pltpu.VMEM((items, frames + 2, rows + 2, cols, channels), jnp.float32),
            pltpu.VMEM(edges, jnp.bfloat16),
            pltpu.VMEM(edges, jnp.bfloat16),
            pltpu.SemaphoreType.DMA((videos,)),
            pltpu.SemaphoreType.DMA((videos,)),
            pltpu.SemaphoreType.DMA((3,)),
            pltpu.SemaphoreType.DMA((items,)),
            pltpu.SemaphoreType.DMA((items,)),
            pltpu.SemaphoreType.DMA((len(SIDES), items)),
            pltpu.SemaphoreType.DMA((len(SIDES), items)),
            pltpu.SemaphoreType.DMA((4 + videos,)),
            pltpu.SemaphoreType.DMA((4 + videos,)),
        ],
        compiler_params=pltpu.CompilerParams(
            collective_id=0, has_side_effects=True, vmem_limit_bytes=58 * 2**20
        ),
    )(
        noise_levels.reshape(1, 1),
        base_frames.reshape((videos,) + flat),
        section_noise.reshape((videos,) + flat),
        spatial_kernel[0],
        temporal_kernel[0],
        output_weight,
    )
    return result.reshape((1,) + base_frames.shape)


def solution(mesh):
    return jax.shard_map(
        on_device,
        mesh=mesh,
        in_specs=(
            P(None, "frames", "space", None, None),
            P("section", None, "frames", "space", None, None),
            P("section"),
            P("section", None, None, None),
            P("section", None, None, None),
            P("section", None, None),
        ),
        out_specs=P("section", None, "frames", "space", None, None),
        check_vma=False,
    )
```

```python
import functools

import jax
import jax.numpy as jnp
from jax import lax
from jax.experimental import pallas as pl
from jax.experimental.pallas import tpu as pltpu
from jax.sharding import PartitionSpec as P

MESH = pl.DeviceIdType.MESH
SIDES = (("frames", 1), ("frames", -1), ("space", 1), ("space", -1))
CHUNK = 4
DEPTH = 2
AHEAD = 2


def kernel(
    videos, ahead, frames, rows, cols, channels,
    level_ref, base_hbm, noise_hbm, spatial_hbm, temporal_hbm, output_hbm, out_ref,
    noise, prior, result, weights, packed, levels, level_out, level_in,
    noisy_ref, middle, edge_out, edge_in,
    noise_sem, base_sem, weight_sem, chain_send, chain_recv, edge_send, edge_recv,
    lend_send, lend_recv,
):
    place = {axis: lax.axis_index(axis) for axis in ("section", "frames", "space")}
    count = {axis: lax.axis_size(axis) for axis in place}

    def has(axis, step):
        return place[axis] < count[axis] - 1 if step > 0 else place[axis] > 0

    def peer(axis, step):
        return {axis: lax.rem(place[axis] + step + count[axis], count[axis])}

    first = place["section"] == 0
    later = jnp.logical_not(first)
    onward = has("section", 1)
    items = videos + ahead
    lag = ahead + 1

    def special(v):
        return jnp.logical_and(v >= videos - lag, v < videos - 1) if ahead else False

    def active(j):
        if not ahead:
            return j < videos
        usual = jnp.logical_and(j < videos, jnp.logical_not(special(j)))
        return jnp.logical_or(usual, jnp.logical_and(first, j < items))

    def load_noise(v):
        return pltpu.make_async_copy(noise_hbm.at[v], noise.at[v], noise_sem.at[v])

    def load_base(v):
        return pltpu.make_async_copy(base_hbm.at[v], prior.at[v], base_sem.at[v])

    def turn(v):
        return v - ahead * (v >= videos - 1).astype(jnp.int32) if ahead else v

    def sent(n):
        return pltpu.make_async_remote_copy(
            src_ref=result.at[0], dst_ref=prior.at[0],
            send_sem=chain_send.at[n], recv_sem=chain_recv.at[n],
            device_id=peer("section", 1), device_id_type=MESH,
        )

    def pass_on(v):
        return pltpu.make_async_remote_copy(
            src_ref=result.at[v], dst_ref=prior.at[v],
            send_sem=chain_send.at[turn(v)], recv_sem=chain_recv.at[turn(v)],
            device_id=peer("section", 1), device_id_type=MESH,
        )

    def finish(j):
        return pltpu.make_async_remote_copy(
            src_ref=result.at[j], dst_ref=out_ref.at[j - lag],
            send_sem=chain_send.at[j - ahead], recv_sem=chain_recv.at[j - ahead],
            device_id=peer("section", 1), device_id_type=MESH,
        )

    def edge(d, v):
        return pltpu.make_async_remote_copy(
            src_ref=edge_out.at[d, v], dst_ref=edge_in.at[d, v],
            send_sem=edge_send.at[d, v], recv_sem=edge_recv.at[d, v],
            device_id=peer(*SIDES[d]), device_id_type=MESH,
        )

    parts = ((spatial_hbm, 0, 9), (temporal_hbm, 9, 3), (output_hbm, 12, 1))
    weight_loads = [
        pltpu.make_async_copy(source, weights.at[0, pl.ds(at, size)], weight_sem.at[n])
        for n, (source, at, size) in enumerate(parts)
    ]
    loans = []
    if ahead:
        pairs = [(level_out, level_in)]
        pairs += [(source, weights.at[1, pl.ds(at, size)]) for source, at, size in parts]
        for v in range(videos - lag, videos - 1):
            pairs.append((noise_hbm.at[v], noise.at[v + lag]))
        loans = [
            pltpu.make_async_remote_copy(
                src_ref=source, dst_ref=target, send_sem=lend_send.at[n], recv_sem=lend_recv.at[n],
                device_id=peer("section", -1), device_id_type=MESH,
            )
            for n, (source, target) in enumerate(pairs)
        ]

    def passes(v):
        if not ahead:
            return onward
        return jnp.logical_and(onward, jnp.logical_and(v < videos, jnp.logical_not(special(v))))

    def sends(v):
        return jnp.logical_or(passes(v), v >= videos)

    neighbours = SIDES + (("section", 1), ("section", -1))
    barrier = pltpu.get_barrier_semaphore()
    for axis, step in neighbours:
        @pl.when(has(axis, step))
        def _():
            pl.semaphore_signal(barrier, inc=1, device_id=peer(axis, step), device_id_type=MESH)

    @pl.loop(0, videos)
    def _(v):
        @pl.when(active(v))
        def _():
            load_noise(v).start()

        @pl.when(first)
        def _():
            load_base(v).start()

    for copy in weight_loads:
        copy.start()

    for d, (axis, step) in enumerate(SIDES):
        @pl.when(jnp.logical_not(has(axis, -step)))
        def _():
            edge_in[d] = jnp.zeros(edge_in.shape[1:], edge_in.dtype)

    levels[0] = jnp.broadcast_to(level_ref[...].astype(jnp.float32), levels.shape[1:])
    level_out[...] = jnp.broadcast_to(level_ref[...], level_out.shape)

    def pack(number):
        packed[number] = jnp.zeros(packed.shape[1:], packed.dtype)
        for a in range(3):
            line = pl.ds(a * channels, channels)
            packed[number, 0, line, :channels] = weights[number, 3 * a + 1]
            packed[number, 0, line, channels:] = weights[number, 3 * a + 2]
            packed[number, 1, line, :channels] = weights[number, 3 * a]
        packed[number, 0, 3 * channels :, :channels] = weights[number, 9]
        packed[number, 1, channels : 2 * channels, channels:] = weights[number, 10]
        packed[number, 1, 3 * channels :, channels:] = weights[number, 11]

    def normalise(v, number):
        noisy = prior[v].astype(jnp.float32) + levels[number][0:1] * noise[v].astype(jnp.float32)
        noisy_ref[v] = noisy
        power = jnp.mean(noisy * noisy, axis=-1, keepdims=True)
        normalized = (noisy * lax.rsqrt(power + 1e-05)).astype(jnp.bfloat16)
        x = normalized.astype(jnp.float32).reshape(frames, rows, cols, channels)
        edge_out[0, v] = normalized[frames - 1]
        edge_out[1, v] = normalized[0]
        edge_out[2, v] = x[:, rows - 1].reshape(frames * cols, channels).astype(jnp.bfloat16)
        edge_out[3, v] = x[:, 0].reshape(frames * cols, channels).astype(jnp.bfloat16)
        middle[v, 1 : 1 + frames, 1 : 1 + rows] = x

    def send_edges(v):
        for d, side in enumerate(SIDES):
            @pl.when(has(*side))
            def _():
                edge(d, v).start()

    def prepare(i):
        @pl.when(i < videos)
        def _():
            load_noise(i).wait()

            @pl.when(first)
            def _():
                load_base(i).wait()

            @pl.when(later)
            def _():
                pass_on(i).wait_recv()

        if ahead:
            @pl.when(i == videos)
            def _():
                for copy in loans:
                    copy.wait_recv()
                levels[1] = level_in[0:8].astype(jnp.float32)
                pack(1)

            @pl.when(i >= videos)
            def _():
                prior[i] = result[i - lag]

        normalise(i, (i >= videos).astype(jnp.int32) if ahead else 0)

    def convolve(v):
        for d, (axis, step) in enumerate(SIDES):
            @pl.when(has(axis, -step))
            def _():
                edge(d, v).wait_recv()
        number = (v >= videos).astype(jnp.int32) if ahead else 0
        middle[v, 0, 1 : 1 + rows] = edge_in[0, v].astype(jnp.float32).reshape(rows, cols, channels)
        middle[v, frames + 1, 1 : 1 + rows] = (
            edge_in[1, v].astype(jnp.float32).reshape(rows, cols, channels)
        )
        for d, at in ((2, 0), (3, rows + 1)):
            middle[v, 1 : 1 + frames, at] = (
                edge_in[d, v].astype(jnp.float32).reshape(frames, cols, channels)
            )
        projection = weights[number, 12]
        level = levels[number][0:1]
        lines = CHUNK * rows
        column = lax.broadcasted_iota(jnp.int32, (lines, cols, channels), 1)
        for f in range(0, frames, CHUNK):
            views = [middle[v, f + 1 : f + 1 + CHUNK, a : a + rows] for a in range(3)]
            views += [middle[v, f + t : f + t + CHUNK, 1 : 1 + rows] for t in (0, 2)]
            views = [view.reshape(-1, channels).astype(jnp.bfloat16) for view in views]
            sums = [
                jnp.dot(
                    jnp.concatenate(views[:3] + [views[3 + n]], axis=-1), packed[number, n],
                    preferred_element_type=jnp.float32,
                )
                for n in range(2)
            ]
            ahead_part = sums[0][:, channels:].reshape(lines, cols, channels)
            behind_part = sums[1][:, :channels].reshape(lines, cols, channels)
            shifted = jnp.where(column == cols - 1, 0.0, pltpu.roll(ahead_part, cols - 1, 1))
            shifted = shifted + jnp.where(column == 0, 0.0, pltpu.roll(behind_part, 1, 1))
            pre = sums[0][:, :channels] + sums[1][:, channels:] + shifted.reshape(-1, channels)
            activated = (pre / (1.0 + jnp.exp(-pre))).astype(jnp.bfloat16)
            estimate = jnp.dot(activated, projection, preferred_element_type=jnp.float32)
            held = noisy_ref[v, f : f + CHUNK]
            result[v, f : f + CHUNK] = (held - level * estimate.reshape(held.shape)).astype(
                jnp.bfloat16
            )

        @pl.when(jnp.logical_and(turn(v) >= DEPTH, sends(v)))
        def _():
            sent(turn(v) - DEPTH).wait_send()

        @pl.when(passes(v))
        def _():
            pass_on(v).start()

        if ahead:
            @pl.when(v >= videos)
            def _():
                finish(v).start()

        @pl.when(v < videos)
        def _():
            out_ref[v] = result[v]

    @pl.when(first)
    def _():
        load_noise(0).wait()
        load_base(0).wait()
        normalise(0, 0)

    pl.semaphore_wait(barrier, sum(has(*side).astype(jnp.int32) for side in neighbours))

    @pl.when(first)
    def _():
        send_edges(0)

    if ahead:
        @pl.when(later)
        def _():
            for copy in loans:
                copy.start()

    @pl.loop(0, items + 1)
    def _(i):
        @pl.when(jnp.logical_and(active(i), jnp.logical_or(i > 0, later)))
        def _():
            prepare(i)
            send_edges(i)

        @pl.when(i == 1)
        def _():
            for copy in weight_loads:
                copy.wait()
            pack(0)

        @pl.when(jnp.logical_and(i > 0, active(i - 1)))
        def _():
            convolve(i - 1)

    @pl.loop(0, items)
    def _(j):
        @pl.when(active(j))
        def _():
            for d, side in enumerate(SIDES):
                @pl.when(has(*side))
                def _():
                    edge(d, j).wait_send()

    @pl.when(onward)
    def _():
        for n in range(max(videos - DEPTH, 0), videos):
            sent(n).wait_send()

    if ahead:
        @pl.when(later)
        def _():
            for copy in loans:
                copy.wait_send()
            for j in range(videos, items):
                finish(j).wait_recv()


def on_device(
    base_frames, section_noise, noise_levels, spatial_kernel, temporal_kernel, output_weight
):
    videos, frames, rows, cols, channels = base_frames.shape
    ahead = AHEAD if lax.axis_size("section") == 2 and videos > AHEAD + 1 else 0
    items = videos + ahead
    flat = (frames, rows * cols, channels)
    edges = (len(SIDES), items, frames * cols, channels)
    assert frames == rows and frames % CHUNK == 0
    result = pl.pallas_call(
        functools.partial(kernel, videos, ahead, frames, rows, cols, channels),
        out_shape=pltpu.VMEM((videos,) + flat, jnp.bfloat16),
        in_specs=[pl.BlockSpec(memory_space=pltpu.VMEM)] + [pl.BlockSpec(memory_space=pltpu.HBM)] * 5,
        out_specs=pl.BlockSpec(memory_space=pltpu.VMEM),
        scratch_shapes=[
            pltpu.VMEM((items,) + flat, jnp.bfloat16),
            pltpu.VMEM((items,) + flat, jnp.bfloat16),
            pltpu.VMEM((items,) + flat, jnp.bfloat16),
            pltpu.VMEM((1 + ahead, 13, channels, channels), jnp.bfloat16),
            pltpu.VMEM((1 + ahead, 2, 4 * channels, 2 * channels), jnp.bfloat16),
            pltpu.VMEM((1 + ahead, 8, channels), jnp.float32),
            pltpu.VMEM((16, channels), jnp.bfloat16),
            pltpu.VMEM((16, channels), jnp.bfloat16),
            pltpu.VMEM((items,) + flat, jnp.float32),
            pltpu.VMEM((items, frames + 2, rows + 2, cols, channels), jnp.float32),
            pltpu.VMEM(edges, jnp.bfloat16),
            pltpu.VMEM(edges, jnp.bfloat16),
            pltpu.SemaphoreType.DMA((videos,)),
            pltpu.SemaphoreType.DMA((videos,)),
            pltpu.SemaphoreType.DMA((3,)),
            pltpu.SemaphoreType.DMA((items,)),
            pltpu.SemaphoreType.DMA((items,)),
            pltpu.SemaphoreType.DMA((len(SIDES), items)),
            pltpu.SemaphoreType.DMA((len(SIDES), items)),
            pltpu.SemaphoreType.DMA((4 + videos,)),
            pltpu.SemaphoreType.DMA((4 + videos,)),
        ],
        compiler_params=pltpu.CompilerParams(
            collective_id=0, has_side_effects=True, vmem_limit_bytes=58 * 2**20
        ),
    )(
        noise_levels.reshape(1, 1),
        base_frames.reshape((videos,) + flat),
        section_noise.reshape((videos,) + flat),
        spatial_kernel[0],
        temporal_kernel[0],
        output_weight,
    )
    return result.reshape((1,) + base_frames.shape)


def solution(mesh):
    return jax.shard_map(
        on_device,
        mesh=mesh,
        in_specs=(
            P(None, "frames", "space", None, None),
            P("section", None, "frames", "space", None, None),
            P("section"),
            P("section", None, None, None),
            P("section", None, None, None),
            P("section", None, None),
        ),
        out_specs=P("section", None, "frames", "space", None, None),
        check_vma=False,
    )
```

```python
import functools

import jax
import jax.numpy as jnp
from jax import lax
from jax.experimental import pallas as pl
from jax.experimental.pallas import tpu as pltpu
from jax.sharding import PartitionSpec as P

MESH = pl.DeviceIdType.MESH
SIDES = (("frames", 1), ("frames", -1), ("space", 1), ("space", -1))
CHUNK = 4
DEPTH = 2
AHEAD = 2
EARLY = 2
MARGIN = 16
PIECES = 5


def kernel(
    videos, ahead, early, frames, rows, cols, channels,
    level_ref, base_hbm, noise_hbm, spatial_hbm, temporal_hbm, output_hbm, out_ref,
    noise, prior, result, weights, packed, levels, level_out, level_in,
    noisy_ref, middle, edge_out, edge_in, inner,
    noise_sem, base_sem, weight_sem, chain_send, chain_recv, edge_send, edge_recv,
    lend_send, lend_recv, piece_send, piece_recv,
):
    place = {axis: lax.axis_index(axis) for axis in ("section", "frames", "space")}
    count = {axis: lax.axis_size(axis) for axis in place}

    def has(axis, step):
        return place[axis] < count[axis] - 1 if step > 0 else place[axis] > 0

    def peer(axis, step):
        return {axis: lax.rem(place[axis] + step + count[axis], count[axis])}

    first = place["section"] == 0
    later = jnp.logical_not(first)
    onward = has("section", 1)
    items = videos + ahead
    lag = ahead + 1

    def special(v):
        return jnp.logical_and(v >= videos - lag, v < videos - 1) if ahead else False

    def active(j):
        if not ahead:
            return j < videos
        usual = jnp.logical_and(j < videos, jnp.logical_not(special(j)))
        return jnp.logical_or(usual, jnp.logical_and(first, j < items))

    def load_noise(v):
        return pltpu.make_async_copy(noise_hbm.at[v], noise.at[v], noise_sem.at[v])

    def load_base(v):
        return pltpu.make_async_copy(base_hbm.at[v], prior.at[v], base_sem.at[v])

    def turn(v):
        return v - ahead * (v >= videos - 1).astype(jnp.int32) if ahead else v

    def sent(n):
        return pltpu.make_async_remote_copy(
            src_ref=result.at[0], dst_ref=prior.at[0],
            send_sem=chain_send.at[n], recv_sem=chain_recv.at[n],
            device_id=peer("section", 1), device_id_type=MESH,
        )

    def pass_on(v):
        return pltpu.make_async_remote_copy(
            src_ref=result.at[v], dst_ref=prior.at[v],
            send_sem=chain_send.at[turn(v)], recv_sem=chain_recv.at[turn(v)],
            device_id=peer("section", 1), device_id_type=MESH,
        )

    def piece(v, n):
        core = pl.ds(MARGIN, rows * cols - 2 * MARGIN)
        part = (
            (pl.ds(1, frames - 2), core),
            (pl.ds(0, frames), pl.ds(0, MARGIN)),
            (pl.ds(0, frames), pl.ds(rows * cols - MARGIN, MARGIN)),
            (pl.ds(0, 1), core),
            (pl.ds(frames - 1, 1), core),
        )[n]
        source = inner if n == 0 else result
        return pltpu.make_async_remote_copy(
            src_ref=source.at[v, part[0], part[1]], dst_ref=prior.at[v, part[0], part[1]],
            send_sem=piece_send.at[v, n], recv_sem=piece_recv.at[v, n],
            device_id=peer("section", 1), device_id_type=MESH,
        )

    def finish(j):
        return pltpu.make_async_remote_copy(
            src_ref=result.at[j], dst_ref=out_ref.at[j - lag],
            send_sem=chain_send.at[j - ahead], recv_sem=chain_recv.at[j - ahead],
            device_id=peer("section", 1), device_id_type=MESH,
        )

    def edge(d, v):
        return pltpu.make_async_remote_copy(
            src_ref=edge_out.at[d, v], dst_ref=edge_in.at[d, v],
            send_sem=edge_send.at[d, v], recv_sem=edge_recv.at[d, v],
            device_id=peer(*SIDES[d]), device_id_type=MESH,
        )

    parts = ((spatial_hbm, 0, 9), (temporal_hbm, 9, 3), (output_hbm, 12, 1))
    weight_loads = [
        pltpu.make_async_copy(source, weights.at[0, pl.ds(at, size)], weight_sem.at[n])
        for n, (source, at, size) in enumerate(parts)
    ]
    loans = []
    if ahead:
        pairs = [(level_out, level_in)]
        pairs += [(source, weights.at[1, pl.ds(at, size)]) for source, at, size in parts]
        for v in range(videos - lag, videos - 1):
            pairs.append((noise_hbm.at[v], noise.at[v + lag]))
        loans = [
            pltpu.make_async_remote_copy(
                src_ref=source, dst_ref=target, send_sem=lend_send.at[n], recv_sem=lend_recv.at[n],
                device_id=peer("section", -1), device_id_type=MESH,
            )
            for n, (source, target) in enumerate(pairs)
        ]

    def passes(v):
        if not ahead:
            return onward
        return jnp.logical_and(onward, jnp.logical_and(v < videos, jnp.logical_not(special(v))))

    def sends(v):
        return jnp.logical_or(passes(v), v >= videos)

    neighbours = SIDES + (("section", 1), ("section", -1))
    barrier = pltpu.get_barrier_semaphore()
    for axis, step in neighbours:
        @pl.when(has(axis, step))
        def _():
            pl.semaphore_signal(barrier, inc=1, device_id=peer(axis, step), device_id_type=MESH)

    @pl.loop(0, videos)
    def _(v):
        @pl.when(active(v))
        def _():
            load_noise(v).start()

        @pl.when(first)
        def _():
            load_base(v).start()

    for copy in weight_loads:
        copy.start()

    for d, (axis, step) in enumerate(SIDES):
        @pl.when(jnp.logical_not(has(axis, -step)))
        def _():
            edge_in[d] = jnp.zeros(edge_in.shape[1:], edge_in.dtype)

    levels[0] = jnp.broadcast_to(level_ref[...].astype(jnp.float32), levels.shape[1:])
    level_out[...] = jnp.broadcast_to(level_ref[...], level_out.shape)

    def pack(number):
        packed[number] = jnp.zeros(packed.shape[1:], packed.dtype)
        for a in range(3):
            line = pl.ds(a * channels, channels)
            packed[number, 0, line, :channels] = weights[number, 3 * a + 1]
            packed[number, 0, line, channels:] = weights[number, 3 * a + 2]
            packed[number, 1, line, :channels] = weights[number, 3 * a]
        packed[number, 0, 3 * channels :, :channels] = weights[number, 9]
        packed[number, 1, channels : 2 * channels, channels:] = weights[number, 10]
        packed[number, 1, 3 * channels :, channels:] = weights[number, 11]

    def normalise(v, number):
        noisy = prior[v].astype(jnp.float32) + levels[number][0:1] * noise[v].astype(jnp.float32)
        noisy_ref[v] = noisy
        power = jnp.mean(noisy * noisy, axis=-1, keepdims=True)
        normalized = (noisy * lax.rsqrt(power + 1e-05)).astype(jnp.bfloat16)
        x = normalized.astype(jnp.float32).reshape(frames, rows, cols, channels)
        edge_out[0, v] = normalized[frames - 1]
        edge_out[1, v] = normalized[0]
        edge_out[2, v] = x[:, rows - 1].reshape(frames * cols, channels).astype(jnp.bfloat16)
        edge_out[3, v] = x[:, 0].reshape(frames * cols, channels).astype(jnp.bfloat16)
        middle[v, 1 : 1 + frames, 1 : 1 + rows] = x

    def send_edges(v):
        for d, side in enumerate(SIDES):
            @pl.when(has(*side))
            def _():
                edge(d, v).start()

    def prepare(i):
        @pl.when(i < videos)
        def _():
            load_noise(i).wait()

            @pl.when(first)
            def _():
                load_base(i).wait()

            if early:
                second = place["section"] == 1
                for v in range(early):
                    @pl.when(jnp.logical_and(second, i == v))
                    def _():
                        for n in range(PIECES):
                            piece(v, n).wait_recv()

                whole = jnp.logical_or(place["section"] > 1, jnp.logical_and(second, i >= early))
            else:
                whole = later

            @pl.when(whole)
            def _():
                pass_on(i).wait_recv()

        if ahead:
            @pl.when(i == videos)
            def _():
                for copy in loans:
                    copy.wait_recv()
                levels[1] = level_in[0:8].astype(jnp.float32)
                pack(1)

            @pl.when(i >= videos)
            def _():
                prior[i] = result[i - lag]

        normalise(i, (i >= videos).astype(jnp.int32) if ahead else 0)

    def estimate_into(target, v, number):
        projection = weights[number, 12]
        level = levels[number][0:1]
        lines = CHUNK * rows
        column = lax.broadcasted_iota(jnp.int32, (lines, cols, channels), 1)
        for f in range(0, frames, CHUNK):
            views = [middle[v, f + 1 : f + 1 + CHUNK, a : a + rows] for a in range(3)]
            views += [middle[v, f + t : f + t + CHUNK, 1 : 1 + rows] for t in (0, 2)]
            views = [view.reshape(-1, channels).astype(jnp.bfloat16) for view in views]
            sums = [
                jnp.dot(
                    jnp.concatenate(views[:3] + [views[3 + n]], axis=-1), packed[number, n],
                    preferred_element_type=jnp.float32,
                )
                for n in range(2)
            ]
            ahead_part = sums[0][:, channels:].reshape(lines, cols, channels)
            behind_part = sums[1][:, :channels].reshape(lines, cols, channels)
            shifted = jnp.where(column == cols - 1, 0.0, pltpu.roll(ahead_part, cols - 1, 1))
            shifted = shifted + jnp.where(column == 0, 0.0, pltpu.roll(behind_part, 1, 1))
            pre = sums[0][:, :channels] + sums[1][:, channels:] + shifted.reshape(-1, channels)
            activated = (pre / (1.0 + jnp.exp(-pre))).astype(jnp.bfloat16)
            estimate = jnp.dot(activated, projection, preferred_element_type=jnp.float32)
            held = noisy_ref[v, f : f + CHUNK]
            target[v, f : f + CHUNK] = (held - level * estimate.reshape(held.shape)).astype(
                jnp.bfloat16
            )

    def convolve(v):
        for d, (axis, step) in enumerate(SIDES):
            @pl.when(has(axis, -step))
            def _():
                edge(d, v).wait_recv()
        number = (v >= videos).astype(jnp.int32) if ahead else 0
        middle[v, 0, 1 : 1 + rows] = edge_in[0, v].astype(jnp.float32).reshape(rows, cols, channels)
        middle[v, frames + 1, 1 : 1 + rows] = (
            edge_in[1, v].astype(jnp.float32).reshape(rows, cols, channels)
        )
        for d, at in ((2, 0), (3, rows + 1)):
            middle[v, 1 : 1 + frames, at] = (
                edge_in[d, v].astype(jnp.float32).reshape(frames, cols, channels)
            )
        estimate_into(result, v, number)

        wholes = jnp.where(first, early, 0)

        @pl.when(jnp.logical_and(turn(v) >= DEPTH + wholes, sends(v)))
        def _():
            sent(turn(v) - DEPTH).wait_send()

        for w in range(early):
            @pl.when(jnp.logical_and(first, v == w))
            def _():
                for n in range(1, PIECES):
                    piece(w, n).start()

        @pl.when(jnp.logical_and(passes(v), v >= wholes))
        def _():
            pass_on(v).start()

        if ahead:
            @pl.when(v >= videos)
            def _():
                finish(v).start()

        @pl.when(v < videos)
        def _():
            out_ref[v] = result[v]

    for copy in weight_loads:
        copy.wait()
    pack(0)

    def start(v):
        load_noise(v).wait()
        load_base(v).wait()
        normalise(v, 0)

    @pl.when(first)
    def _():
        start(0)
        if early:
            estimate_into(inner, 0, 0)

    pl.semaphore_wait(barrier, sum(has(*side).astype(jnp.int32) for side in neighbours))

    @pl.when(first)
    def _():
        send_edges(0)
        if early:
            piece(0, 0).start()
        for v in range(1, early):
            start(v)
            send_edges(v)
            estimate_into(inner, v, 0)
            piece(v, 0).start()

    if ahead:
        @pl.when(later)
        def _():
            for copy in loans:
                copy.start()

    @pl.loop(0, items + 1)
    def _(i):
        @pl.when(jnp.logical_and(active(i), jnp.logical_or(i >= max(early, 1), later)))
        def _():
            prepare(i)
            send_edges(i)

        @pl.when(jnp.logical_and(i > 0, active(i - 1)))
        def _():
            convolve(i - 1)

    @pl.loop(0, items)
    def _(j):
        @pl.when(active(j))
        def _():
            for d, side in enumerate(SIDES):
                @pl.when(has(*side))
                def _():
                    edge(d, j).wait_send()

    if early:
        @pl.when(first)
        def _():
            for v in range(early):
                for n in range(PIECES):
                    piece(v, n).wait_send()

    @pl.when(onward)
    def _():
        for n in range(max(videos - DEPTH, 0), videos):
            sent(n).wait_send()

    if ahead:
        @pl.when(later)
        def _():
            for copy in loans:
                copy.wait_send()
            for j in range(videos, items):
                finish(j).wait_recv()


def on_device(
    base_frames, section_noise, noise_levels, spatial_kernel, temporal_kernel, output_weight
):
    videos, frames, rows, cols, channels = base_frames.shape
    ahead = AHEAD if lax.axis_size("section") == 2 and videos > AHEAD + 1 else 0
    early = EARLY if lax.axis_size("section") > 1 and videos >= EARLY + DEPTH + ahead else 0
    items = videos + ahead
    flat = (frames, rows * cols, channels)
    edges = (len(SIDES), items, frames * cols, channels)
    assert frames == rows and frames % CHUNK == 0 and MARGIN % cols == 0
    assert rows * cols > 2 * MARGIN and frames > 2
    result = pl.pallas_call(
        functools.partial(kernel, videos, ahead, early, frames, rows, cols, channels),
        out_shape=pltpu.VMEM((videos,) + flat, jnp.bfloat16),
        in_specs=[pl.BlockSpec(memory_space=pltpu.VMEM)] + [pl.BlockSpec(memory_space=pltpu.HBM)] * 5,
        out_specs=pl.BlockSpec(memory_space=pltpu.VMEM),
        scratch_shapes=[
            pltpu.VMEM((items,) + flat, jnp.bfloat16),
            pltpu.VMEM((items,) + flat, jnp.bfloat16),
            pltpu.VMEM((items,) + flat, jnp.bfloat16),
            pltpu.VMEM((1 + ahead, 13, channels, channels), jnp.bfloat16),
            pltpu.VMEM((1 + ahead, 2, 4 * channels, 2 * channels), jnp.bfloat16),
            pltpu.VMEM((1 + ahead, 8, channels), jnp.float32),
            pltpu.VMEM((16, channels), jnp.bfloat16),
            pltpu.VMEM((16, channels), jnp.bfloat16),
            pltpu.VMEM((items,) + flat, jnp.float32),
            pltpu.VMEM((items, frames + 2, rows + 2, cols, channels), jnp.float32),
            pltpu.VMEM(edges, jnp.bfloat16),
            pltpu.VMEM(edges, jnp.bfloat16),
            pltpu.VMEM((EARLY,) + flat, jnp.bfloat16),
            pltpu.SemaphoreType.DMA((videos,)),
            pltpu.SemaphoreType.DMA((videos,)),
            pltpu.SemaphoreType.DMA((3,)),
            pltpu.SemaphoreType.DMA((items,)),
            pltpu.SemaphoreType.DMA((items,)),
            pltpu.SemaphoreType.DMA((len(SIDES), items)),
            pltpu.SemaphoreType.DMA((len(SIDES), items)),
            pltpu.SemaphoreType.DMA((4 + videos,)),
            pltpu.SemaphoreType.DMA((4 + videos,)),
            pltpu.SemaphoreType.DMA((EARLY, PIECES)),
            pltpu.SemaphoreType.DMA((EARLY, PIECES)),
        ],
        compiler_params=pltpu.CompilerParams(
            collective_id=0, has_side_effects=True, vmem_limit_bytes=58 * 2**20
        ),
    )(
        noise_levels.reshape(1, 1),
        base_frames.reshape((videos,) + flat),
        section_noise.reshape((videos,) + flat),
        spatial_kernel[0],
        temporal_kernel[0],
        output_weight,
    )
    return result.reshape((1,) + base_frames.shape)


def solution(mesh):
    return jax.shard_map(
        on_device,
        mesh=mesh,
        in_specs=(
            P(None, "frames", "space", None, None),
            P("section", None, "frames", "space", None, None),
            P("section"),
            P("section", None, None, None),
            P("section", None, None, None),
            P("section", None, None),
        ),
        out_specs=P("section", None, "frames", "space", None, None),
        check_vma=False,
    )
```

```python
import functools

import jax
import jax.numpy as jnp
from jax import lax
from jax.experimental import pallas as pl
from jax.experimental.pallas import tpu as pltpu
from jax.sharding import PartitionSpec as P

MESH = pl.DeviceIdType.MESH
SIDES = (("frames", 1), ("frames", -1), ("space", 1), ("space", -1))
CHUNK = 4
DEPTH = 2
AHEAD = 2
EARLY = 1
MARGIN = 16
PIECES = 5


def kernel(
    videos, ahead, early, frames, rows, cols, channels,
    level_ref, base_hbm, noise_hbm, spatial_hbm, temporal_hbm, output_hbm, out_ref,
    noise, prior, result, weights, packed, levels, level_out, level_in,
    noisy_ref, middle, edge_out, edge_in, inner,
    noise_sem, base_sem, weight_sem, chain_send, chain_recv, edge_send, edge_recv,
    lend_send, lend_recv, piece_send, piece_recv,
):
    place = {axis: lax.axis_index(axis) for axis in ("section", "frames", "space")}
    count = {axis: lax.axis_size(axis) for axis in place}

    around = {
        (axis, step): jnp.clip(place[axis] + step, 0, count[axis] - 1)
        for axis in place
        for step in (1, -1)
    }
    exists = {
        (axis, step): place[axis] < count[axis] - 1 if step > 0 else place[axis] > 0
        for axis, step in around
    }

    def has(axis, step):
        return exists[axis, step]

    def peer(axis, step):
        return {axis: around[axis, step]}

    first = place["section"] == 0
    later = jnp.logical_not(first)
    onward = has("section", 1)
    items = videos + ahead
    lag = ahead + 1

    def special(v):
        return jnp.logical_and(v >= videos - lag, v < videos - 1) if ahead else False

    def active(j):
        if not ahead:
            return j < videos
        usual = jnp.logical_and(j < videos, jnp.logical_not(special(j)))
        return jnp.logical_or(usual, jnp.logical_and(first, j < items))

    def load_noise(v):
        return pltpu.make_async_copy(noise_hbm.at[v], noise.at[v], noise_sem.at[v])

    def load_base(v):
        return pltpu.make_async_copy(base_hbm.at[v], prior.at[v], base_sem.at[v])

    def turn(v):
        return v - ahead * (v >= videos - 1).astype(jnp.int32) if ahead else v

    def sent(n):
        return pltpu.make_async_remote_copy(
            src_ref=result.at[0], dst_ref=prior.at[0],
            send_sem=chain_send.at[n], recv_sem=chain_recv.at[n],
            device_id=peer("section", 1), device_id_type=MESH,
        )

    def pass_on(v):
        return pltpu.make_async_remote_copy(
            src_ref=result.at[v], dst_ref=prior.at[v],
            send_sem=chain_send.at[turn(v)], recv_sem=chain_recv.at[turn(v)],
            device_id=peer("section", 1), device_id_type=MESH,
        )

    def piece(v, n):
        core = pl.ds(MARGIN, rows * cols - 2 * MARGIN)
        part = (
            (pl.ds(1, frames - 2), core),
            (pl.ds(0, frames), pl.ds(0, MARGIN)),
            (pl.ds(0, frames), pl.ds(rows * cols - MARGIN, MARGIN)),
            (pl.ds(0, 1), core),
            (pl.ds(frames - 1, 1), core),
        )[n]
        source = inner if n == 0 else result
        return pltpu.make_async_remote_copy(
            src_ref=source.at[v, part[0], part[1]], dst_ref=prior.at[v, part[0], part[1]],
            send_sem=piece_send.at[v, n], recv_sem=piece_recv.at[v, n],
            device_id=peer("section", 1), device_id_type=MESH,
        )

    def finish(j):
        return pltpu.make_async_remote_copy(
            src_ref=result.at[j], dst_ref=out_ref.at[j - lag],
            send_sem=chain_send.at[j - ahead], recv_sem=chain_recv.at[j - ahead],
            device_id=peer("section", 1), device_id_type=MESH,
        )

    def edge(d, v):
        return pltpu.make_async_remote_copy(
            src_ref=edge_out.at[d, v], dst_ref=edge_in.at[d, v],
            send_sem=edge_send.at[d, v], recv_sem=edge_recv.at[d, v],
            device_id=peer(*SIDES[d]), device_id_type=MESH,
        )

    parts = ((spatial_hbm, 0, 9), (temporal_hbm, 9, 3), (output_hbm, 12, 1))
    weight_loads = [
        pltpu.make_async_copy(source, weights.at[0, pl.ds(at, size)], weight_sem.at[n])
        for n, (source, at, size) in enumerate(parts)
    ]
    loans = []
    if ahead:
        pairs = [(level_out, level_in)]
        pairs += [(source, weights.at[1, pl.ds(at, size)]) for source, at, size in parts]
        for v in range(videos - lag, videos - 1):
            pairs.append((noise_hbm.at[v], noise.at[v + lag]))
        loans = [
            pltpu.make_async_remote_copy(
                src_ref=source, dst_ref=target, send_sem=lend_send.at[n], recv_sem=lend_recv.at[n],
                device_id=peer("section", -1), device_id_type=MESH,
            )
            for n, (source, target) in enumerate(pairs)
        ]

    def passes(v):
        if not ahead:
            return onward
        return jnp.logical_and(onward, jnp.logical_and(v < videos, jnp.logical_not(special(v))))

    def sends(v):
        return jnp.logical_or(passes(v), v >= videos)

    neighbours = SIDES + (("section", 1), ("section", -1))
    barrier = pltpu.get_barrier_semaphore()
    for axis, step in neighbours:
        @pl.when(has(axis, step))
        def _():
            pl.semaphore_signal(barrier, inc=1, device_id=peer(axis, step), device_id_type=MESH)

    @pl.loop(0, videos)
    def _(v):
        @pl.when(active(v))
        def _():
            load_noise(v).start()

        @pl.when(first)
        def _():
            load_base(v).start()

    for copy in weight_loads:
        copy.start()

    for d, (axis, step) in enumerate(SIDES):
        @pl.when(jnp.logical_not(has(axis, -step)))
        def _():
            edge_in[d] = jnp.zeros(edge_in.shape[1:], edge_in.dtype)

    levels[0] = jnp.broadcast_to(level_ref[...].astype(jnp.float32), levels.shape[1:])
    level_out[...] = jnp.broadcast_to(level_ref[...], level_out.shape)

    def pack(number):
        packed[number] = jnp.zeros(packed.shape[1:], packed.dtype)
        for a in range(3):
            line = pl.ds(a * channels, channels)
            packed[number, 0, line, :channels] = weights[number, 3 * a + 1]
            packed[number, 0, line, channels:] = weights[number, 3 * a + 2]
            packed[number, 1, line, :channels] = weights[number, 3 * a]
        packed[number, 0, 3 * channels :, :channels] = weights[number, 9]
        packed[number, 1, channels : 2 * channels, channels:] = weights[number, 10]
        packed[number, 1, 3 * channels :, channels:] = weights[number, 11]

    def normalise(v, number):
        noisy = prior[v].astype(jnp.float32) + levels[number][0:1] * noise[v].astype(jnp.float32)
        noisy_ref[v] = noisy
        power = jnp.mean(noisy * noisy, axis=-1, keepdims=True)
        normalized = (noisy * lax.rsqrt(power + 1e-05)).astype(jnp.bfloat16)
        x = normalized.astype(jnp.float32).reshape(frames, rows, cols, channels)
        edge_out[0, v] = normalized[frames - 1]
        edge_out[1, v] = normalized[0]
        edge_out[2, v] = x[:, rows - 1].reshape(frames * cols, channels).astype(jnp.bfloat16)
        edge_out[3, v] = x[:, 0].reshape(frames * cols, channels).astype(jnp.bfloat16)
        middle[v, 1 : 1 + frames, 1 : 1 + rows] = x

    def send_edges(v):
        for d, side in enumerate(SIDES):
            @pl.when(has(*side))
            def _():
                edge(d, v).start()

    def prepare(i):
        @pl.when(i < videos)
        def _():
            load_noise(i).wait()

            @pl.when(first)
            def _():
                load_base(i).wait()

            if early:
                second = place["section"] == 1
                for v in range(early):
                    @pl.when(jnp.logical_and(second, i == v))
                    def _():
                        for n in range(PIECES):
                            piece(v, n).wait_recv()

                whole = jnp.logical_or(place["section"] > 1, jnp.logical_and(second, i >= early))
            else:
                whole = later

            @pl.when(whole)
            def _():
                pass_on(i).wait_recv()

        if ahead:
            @pl.when(i == videos)
            def _():
                for copy in loans:
                    copy.wait_recv()
                levels[1] = level_in[0:8].astype(jnp.float32)
                pack(1)

            @pl.when(i >= videos)
            def _():
                prior[i] = result[i - lag]

        normalise(i, (i >= videos).astype(jnp.int32) if ahead else 0)

    def estimate_into(target, v, number):
        projection = weights[number, 12]
        level = levels[number][0:1]
        lines = CHUNK * rows
        column = lax.broadcasted_iota(jnp.int32, (lines, cols, channels), 1)
        for f in range(0, frames, CHUNK):
            views = [middle[v, f + 1 : f + 1 + CHUNK, a : a + rows] for a in range(3)]
            views += [middle[v, f + t : f + t + CHUNK, 1 : 1 + rows] for t in (0, 2)]
            views = [view.reshape(-1, channels).astype(jnp.bfloat16) for view in views]
            sums = [
                jnp.dot(
                    jnp.concatenate(views[:3] + [views[3 + n]], axis=-1), packed[number, n],
                    preferred_element_type=jnp.float32,
                )
                for n in range(2)
            ]
            ahead_part = sums[0][:, channels:].reshape(lines, cols, channels)
            behind_part = sums[1][:, :channels].reshape(lines, cols, channels)
            shifted = jnp.where(column == cols - 1, 0.0, pltpu.roll(ahead_part, cols - 1, 1))
            shifted = shifted + jnp.where(column == 0, 0.0, pltpu.roll(behind_part, 1, 1))
            pre = sums[0][:, :channels] + sums[1][:, channels:] + shifted.reshape(-1, channels)
            activated = (0.5 * pre * (1.0 + jnp.tanh(0.5 * pre))).astype(jnp.bfloat16)
            estimate = jnp.dot(activated, projection, preferred_element_type=jnp.float32)
            held = noisy_ref[v, f : f + CHUNK]
            target[v, f : f + CHUNK] = (held - level * estimate.reshape(held.shape)).astype(
                jnp.bfloat16
            )

    def convolve(v):
        for d, (axis, step) in enumerate(SIDES):
            @pl.when(has(axis, -step))
            def _():
                edge(d, v).wait_recv()
        number = (v >= videos).astype(jnp.int32) if ahead else 0
        middle[v, 0, 1 : 1 + rows] = edge_in[0, v].astype(jnp.float32).reshape(rows, cols, channels)
        middle[v, frames + 1, 1 : 1 + rows] = (
            edge_in[1, v].astype(jnp.float32).reshape(rows, cols, channels)
        )
        for d, at in ((2, 0), (3, rows + 1)):
            middle[v, 1 : 1 + frames, at] = (
                edge_in[d, v].astype(jnp.float32).reshape(frames, cols, channels)
            )
        estimate_into(result, v, number)

        wholes = jnp.where(first, early, 0)

        @pl.when(jnp.logical_and(turn(v) >= DEPTH + wholes, sends(v)))
        def _():
            sent(turn(v) - DEPTH).wait_send()

        for w in range(early):
            @pl.when(jnp.logical_and(first, v == w))
            def _():
                for n in range(1, PIECES):
                    piece(w, n).start()

        @pl.when(jnp.logical_and(passes(v), v >= wholes))
        def _():
            pass_on(v).start()

        if ahead:
            @pl.when(v >= videos)
            def _():
                finish(v).start()

        @pl.when(v < videos)
        def _():
            out_ref[v] = result[v]

    for copy in weight_loads:
        copy.wait()
    pack(0)

    def start(v):
        load_noise(v).wait()
        load_base(v).wait()
        normalise(v, 0)

    @pl.when(first)
    def _():
        start(0)
        if early:
            estimate_into(inner, 0, 0)

    pl.semaphore_wait(barrier, sum(has(*side).astype(jnp.int32) for side in neighbours))

    @pl.when(first)
    def _():
        send_edges(0)
        if early:
            piece(0, 0).start()
        for v in range(1, early):
            start(v)
            send_edges(v)
            estimate_into(inner, v, 0)
            piece(v, 0).start()

    if ahead:
        @pl.when(later)
        def _():
            for copy in loans:
                copy.start()

    @pl.loop(0, items + 1)
    def _(i):
        @pl.when(jnp.logical_and(active(i), jnp.logical_or(i >= max(early, 1), later)))
        def _():
            prepare(i)
            send_edges(i)

        @pl.when(jnp.logical_and(i > 0, active(i - 1)))
        def _():
            convolve(i - 1)

    @pl.loop(0, items)
    def _(j):
        @pl.when(active(j))
        def _():
            for d, side in enumerate(SIDES):
                @pl.when(has(*side))
                def _():
                    edge(d, j).wait_send()

    if early:
        @pl.when(first)
        def _():
            for v in range(early):
                for n in range(PIECES):
                    piece(v, n).wait_send()

    @pl.when(onward)
    def _():
        for n in range(max(videos - DEPTH, 0), videos):
            sent(n).wait_send()

    if ahead:
        @pl.when(later)
        def _():
            for copy in loans:
                copy.wait_send()
            for j in range(videos, items):
                finish(j).wait_recv()


def on_device(
    base_frames, section_noise, noise_levels, spatial_kernel, temporal_kernel, output_weight
):
    videos, frames, rows, cols, channels = base_frames.shape
    ahead = AHEAD if lax.axis_size("section") == 2 and videos > AHEAD + 1 else 0
    early = EARLY if lax.axis_size("section") > 1 and videos >= EARLY + DEPTH + ahead else 0
    items = videos + ahead
    flat = (frames, rows * cols, channels)
    edges = (len(SIDES), items, frames * cols, channels)
    assert frames == rows and frames % CHUNK == 0 and MARGIN % cols == 0
    assert rows * cols > 2 * MARGIN and frames > 2
    result = pl.pallas_call(
        functools.partial(kernel, videos, ahead, early, frames, rows, cols, channels),
        out_shape=pltpu.VMEM((videos,) + flat, jnp.bfloat16),
        in_specs=[pl.BlockSpec(memory_space=pltpu.VMEM)] + [pl.BlockSpec(memory_space=pltpu.HBM)] * 5,
        out_specs=pl.BlockSpec(memory_space=pltpu.VMEM),
        scratch_shapes=[
            pltpu.VMEM((items,) + flat, jnp.bfloat16),
            pltpu.VMEM((items,) + flat, jnp.bfloat16),
            pltpu.VMEM((items,) + flat, jnp.bfloat16),
            pltpu.VMEM((1 + ahead, 13, channels, channels), jnp.bfloat16),
            pltpu.VMEM((1 + ahead, 2, 4 * channels, 2 * channels), jnp.bfloat16),
            pltpu.VMEM((1 + ahead, 8, channels), jnp.float32),
            pltpu.VMEM((16, channels), jnp.bfloat16),
            pltpu.VMEM((16, channels), jnp.bfloat16),
            pltpu.VMEM((items,) + flat, jnp.float32),
            pltpu.VMEM((items, frames + 2, rows + 2, cols, channels), jnp.float32),
            pltpu.VMEM(edges, jnp.bfloat16),
            pltpu.VMEM(edges, jnp.bfloat16),
            pltpu.VMEM((EARLY,) + flat, jnp.bfloat16),
            pltpu.SemaphoreType.DMA((videos,)),
            pltpu.SemaphoreType.DMA((videos,)),
            pltpu.SemaphoreType.DMA((3,)),
            pltpu.SemaphoreType.DMA((items,)),
            pltpu.SemaphoreType.DMA((items,)),
            pltpu.SemaphoreType.DMA((len(SIDES), items)),
            pltpu.SemaphoreType.DMA((len(SIDES), items)),
            pltpu.SemaphoreType.DMA((4 + videos,)),
            pltpu.SemaphoreType.DMA((4 + videos,)),
            pltpu.SemaphoreType.DMA((EARLY, PIECES)),
            pltpu.SemaphoreType.DMA((EARLY, PIECES)),
        ],
        compiler_params=pltpu.CompilerParams(
            collective_id=0, has_side_effects=True, vmem_limit_bytes=58 * 2**20
        ),
    )(
        noise_levels.reshape(1, 1),
        base_frames.reshape((videos,) + flat),
        section_noise.reshape((videos,) + flat),
        spatial_kernel[0],
        temporal_kernel[0],
        output_weight,
    )
    return result.reshape((1,) + base_frames.shape)


def solution(mesh):
    return jax.shard_map(
        on_device,
        mesh=mesh,
        in_specs=(
            P(None, "frames", "space", None, None),
            P("section", None, "frames", "space", None, None),
            P("section"),
            P("section", None, None, None),
            P("section", None, None, None),
            P("section", None, None),
        ),
        out_specs=P("section", None, "frames", "space", None, None),
        check_vma=False,
    )
```

```python
import functools

import jax
import jax.numpy as jnp
from jax import lax
from jax.experimental import pallas as pl
from jax.experimental.pallas import tpu as pltpu
from jax.sharding import PartitionSpec as P

MESH = pl.DeviceIdType.MESH
SIDES = (("frames", 1), ("frames", -1), ("space", 1), ("space", -1))
CHUNK = 4
DEPTH = 2
AHEAD = 2
LOOK = 3
EARLY = 1
MARGIN = 16
PIECES = 5


def kernel(
    videos, ahead, early, frames, rows, cols, channels,
    level_ref, base_hbm, noise_hbm, spatial_hbm, temporal_hbm, output_hbm, out_ref,
    noise, prior, result, weights, packed, levels, level_out, level_in,
    noisy_ref, middle, edge_out, edge_in, inner,
    noise_sem, base_sem, weight_sem, chain_send, chain_recv, edge_send, edge_recv,
    lend_send, lend_recv, piece_send, piece_recv,
):
    place = {axis: lax.axis_index(axis) for axis in ("section", "frames", "space")}
    count = {axis: lax.axis_size(axis) for axis in place}

    around = {
        (axis, step): jnp.clip(place[axis] + step, 0, count[axis] - 1)
        for axis in place
        for step in (1, -1)
    }
    exists = {
        (axis, step): place[axis] < count[axis] - 1 if step > 0 else place[axis] > 0
        for axis, step in around
    }

    def has(axis, step):
        return exists[axis, step]

    def peer(axis, step):
        return {axis: around[axis, step]}

    first = place["section"] == 0
    later = jnp.logical_not(first)
    onward = has("section", 1)
    items = videos + ahead
    lag = max(ahead, LOOK) + 1
    look = jnp.where(first, LOOK, 1)

    def special(v):
        return jnp.logical_and(v >= videos - lag, v < videos - lag + ahead) if ahead else False

    def active(j):
        if not ahead:
            return j < videos
        usual = jnp.logical_and(j < videos, jnp.logical_not(special(j)))
        return jnp.logical_or(usual, jnp.logical_and(first, j < items))

    def load_noise(v):
        return pltpu.make_async_copy(noise_hbm.at[v], noise.at[v], noise_sem.at[v])

    def load_base(v):
        return pltpu.make_async_copy(base_hbm.at[v], prior.at[v], base_sem.at[v])

    def turn(v):
        return v - ahead * (v >= videos - lag + ahead).astype(jnp.int32) if ahead else v

    def sent(n):
        return pltpu.make_async_remote_copy(
            src_ref=result.at[0], dst_ref=prior.at[0],
            send_sem=chain_send.at[n], recv_sem=chain_recv.at[n],
            device_id=peer("section", 1), device_id_type=MESH,
        )

    def pass_on(v):
        return pltpu.make_async_remote_copy(
            src_ref=result.at[v], dst_ref=prior.at[v],
            send_sem=chain_send.at[turn(v)], recv_sem=chain_recv.at[turn(v)],
            device_id=peer("section", 1), device_id_type=MESH,
        )

    def piece(v, n):
        core = pl.ds(MARGIN, rows * cols - 2 * MARGIN)
        part = (
            (pl.ds(1, frames - 2), core),
            (pl.ds(0, frames), pl.ds(0, MARGIN)),
            (pl.ds(0, frames), pl.ds(rows * cols - MARGIN, MARGIN)),
            (pl.ds(0, 1), core),
            (pl.ds(frames - 1, 1), core),
        )[n]
        source = inner if n == 0 else result
        return pltpu.make_async_remote_copy(
            src_ref=source.at[v, part[0], part[1]], dst_ref=prior.at[v, part[0], part[1]],
            send_sem=piece_send.at[v, n], recv_sem=piece_recv.at[v, n],
            device_id=peer("section", 1), device_id_type=MESH,
        )

    def finish(j):
        return pltpu.make_async_remote_copy(
            src_ref=result.at[j], dst_ref=out_ref.at[j - lag],
            send_sem=chain_send.at[j - ahead], recv_sem=chain_recv.at[j - ahead],
            device_id=peer("section", 1), device_id_type=MESH,
        )

    def edge(d, v):
        return pltpu.make_async_remote_copy(
            src_ref=edge_out.at[d, v], dst_ref=edge_in.at[d, v],
            send_sem=edge_send.at[d, v], recv_sem=edge_recv.at[d, v],
            device_id=peer(*SIDES[d]), device_id_type=MESH,
        )

    parts = ((spatial_hbm, 0, 9), (temporal_hbm, 9, 3), (output_hbm, 12, 1))
    weight_loads = [
        pltpu.make_async_copy(source, weights.at[0, pl.ds(at, size)], weight_sem.at[n])
        for n, (source, at, size) in enumerate(parts)
    ]
    loans = []
    if ahead:
        pairs = [(level_out, level_in)]
        pairs += [(source, weights.at[1, pl.ds(at, size)]) for source, at, size in parts]
        for v in range(videos - lag, videos - lag + ahead):
            pairs.append((noise_hbm.at[v], noise.at[v + lag]))
        loans = [
            pltpu.make_async_remote_copy(
                src_ref=source, dst_ref=target, send_sem=lend_send.at[n], recv_sem=lend_recv.at[n],
                device_id=peer("section", -1), device_id_type=MESH,
            )
            for n, (source, target) in enumerate(pairs)
        ]

    def passes(v):
        if not ahead:
            return onward
        return jnp.logical_and(onward, jnp.logical_and(v < videos, jnp.logical_not(special(v))))

    def sends(v):
        return jnp.logical_or(passes(v), v >= videos)

    neighbours = SIDES + (("section", 1), ("section", -1))
    barrier = pltpu.get_barrier_semaphore()
    for axis, step in neighbours:
        @pl.when(has(axis, step))
        def _():
            pl.semaphore_signal(barrier, inc=1, device_id=peer(axis, step), device_id_type=MESH)

    @pl.loop(0, videos)
    def _(v):
        @pl.when(active(v))
        def _():
            load_noise(v).start()

        @pl.when(first)
        def _():
            load_base(v).start()

    for copy in weight_loads:
        copy.start()

    for d, (axis, step) in enumerate(SIDES):
        @pl.when(jnp.logical_not(has(axis, -step)))
        def _():
            edge_in[d] = jnp.zeros(edge_in.shape[1:], edge_in.dtype)

    levels[0] = jnp.broadcast_to(level_ref[...].astype(jnp.float32), levels.shape[1:])
    level_out[...] = jnp.broadcast_to(level_ref[...], level_out.shape)

    def pack(number):
        packed[number] = jnp.zeros(packed.shape[1:], packed.dtype)
        for a in range(3):
            line = pl.ds(a * channels, channels)
            packed[number, 0, line, :channels] = weights[number, 3 * a + 1]
            packed[number, 0, line, channels:] = weights[number, 3 * a + 2]
            packed[number, 1, line, :channels] = weights[number, 3 * a]
        packed[number, 0, 3 * channels :, :channels] = weights[number, 9]
        packed[number, 1, channels : 2 * channels, channels:] = weights[number, 10]
        packed[number, 1, 3 * channels :, channels:] = weights[number, 11]

    def normalise(v, number):
        noisy = prior[v].astype(jnp.float32) + levels[number][0:1] * noise[v].astype(jnp.float32)
        noisy_ref[v] = noisy
        power = jnp.mean(noisy * noisy, axis=-1, keepdims=True)
        normalized = (noisy * lax.rsqrt(power + 1e-05)).astype(jnp.bfloat16)
        x = normalized.astype(jnp.float32).reshape(frames, rows, cols, channels)
        edge_out[0, v] = normalized[frames - 1]
        edge_out[1, v] = normalized[0]
        edge_out[2, v] = x[:, rows - 1].reshape(frames * cols, channels).astype(jnp.bfloat16)
        edge_out[3, v] = x[:, 0].reshape(frames * cols, channels).astype(jnp.bfloat16)
        middle[v, 1 : 1 + frames, 1 : 1 + rows] = x

    def send_edges(v):
        for d, side in enumerate(SIDES):
            @pl.when(has(*side))
            def _():
                edge(d, v).start()

    def prepare(i):
        @pl.when(i < videos)
        def _():
            load_noise(i).wait()

            @pl.when(first)
            def _():
                load_base(i).wait()

            if early:
                second = place["section"] == 1
                for v in range(early):
                    @pl.when(jnp.logical_and(second, i == v))
                    def _():
                        for n in range(PIECES):
                            piece(v, n).wait_recv()

                whole = jnp.logical_or(place["section"] > 1, jnp.logical_and(second, i >= early))
            else:
                whole = later

            @pl.when(whole)
            def _():
                pass_on(i).wait_recv()

        if ahead:
            @pl.when(i == videos)
            def _():
                for copy in loans:
                    copy.wait_recv()
                levels[1] = level_in[0:8].astype(jnp.float32)
                pack(1)

            @pl.when(i >= videos)
            def _():
                prior[i] = result[i - lag]

        normalise(i, (i >= videos).astype(jnp.int32) if ahead else 0)

    def estimate_into(target, v, number):
        projection = weights[number, 12]
        level = levels[number][0:1]
        lines = CHUNK * rows
        column = lax.broadcasted_iota(jnp.int32, (lines, cols, channels), 1)
        for f in range(0, frames, CHUNK):
            views = [middle[v, f + 1 : f + 1 + CHUNK, a : a + rows] for a in range(3)]
            views += [middle[v, f + t : f + t + CHUNK, 1 : 1 + rows] for t in (0, 2)]
            views = [view.reshape(-1, channels).astype(jnp.bfloat16) for view in views]
            sums = [
                jnp.dot(
                    jnp.concatenate(views[:3] + [views[3 + n]], axis=-1), packed[number, n],
                    preferred_element_type=jnp.float32,
                )
                for n in range(2)
            ]
            ahead_part = sums[0][:, channels:].reshape(lines, cols, channels)
            behind_part = sums[1][:, :channels].reshape(lines, cols, channels)
            shifted = jnp.where(column == cols - 1, 0.0, pltpu.roll(ahead_part, cols - 1, 1))
            shifted = shifted + jnp.where(column == 0, 0.0, pltpu.roll(behind_part, 1, 1))
            pre = sums[0][:, :channels] + sums[1][:, channels:] + shifted.reshape(-1, channels)
            activated = (0.5 * pre * (1.0 + jnp.tanh(0.5 * pre))).astype(jnp.bfloat16)
            estimate = jnp.dot(activated, projection, preferred_element_type=jnp.float32)
            held = noisy_ref[v, f : f + CHUNK]
            target[v, f : f + CHUNK] = (held - level * estimate.reshape(held.shape)).astype(
                jnp.bfloat16
            )

    def convolve(v):
        for d, (axis, step) in enumerate(SIDES):
            @pl.when(has(axis, -step))
            def _():
                edge(d, v).wait_recv()
        number = (v >= videos).astype(jnp.int32) if ahead else 0
        middle[v, 0, 1 : 1 + rows] = edge_in[0, v].astype(jnp.float32).reshape(rows, cols, channels)
        middle[v, frames + 1, 1 : 1 + rows] = (
            edge_in[1, v].astype(jnp.float32).reshape(rows, cols, channels)
        )
        for d, at in ((2, 0), (3, rows + 1)):
            middle[v, 1 : 1 + frames, at] = (
                edge_in[d, v].astype(jnp.float32).reshape(frames, cols, channels)
            )
        estimate_into(result, v, number)

        wholes = jnp.where(first, early, 0)

        @pl.when(jnp.logical_and(turn(v) >= DEPTH + wholes, sends(v)))
        def _():
            sent(turn(v) - DEPTH).wait_send()

        for w in range(early):
            @pl.when(jnp.logical_and(first, v == w))
            def _():
                for n in range(1, PIECES):
                    piece(w, n).start()

        @pl.when(jnp.logical_and(passes(v), v >= wholes))
        def _():
            pass_on(v).start()

        if ahead:
            @pl.when(v >= videos)
            def _():
                finish(v).start()

        @pl.when(v < videos)
        def _():
            out_ref[v] = result[v]

    for copy in weight_loads:
        copy.wait()
    pack(0)

    def start(v):
        load_noise(v).wait()
        load_base(v).wait()
        normalise(v, 0)

    @pl.when(first)
    def _():
        start(0)
        if early:
            estimate_into(inner, 0, 0)

    pl.semaphore_wait(barrier, sum(has(*side).astype(jnp.int32) for side in neighbours))

    @pl.when(first)
    def _():
        send_edges(0)
        if early:
            piece(0, 0).start()
        for v in range(1, early):
            start(v)
            send_edges(v)
            estimate_into(inner, v, 0)
            piece(v, 0).start()

    if ahead:
        @pl.when(later)
        def _():
            for copy in loans:
                copy.start()

    @pl.loop(0, items + LOOK)
    def _(i):
        @pl.when(jnp.logical_and(active(i), jnp.logical_or(i >= max(early, 1), later)))
        def _():
            prepare(i)
            send_edges(i)

        @pl.when(jnp.logical_and(i >= look, active(i - look)))
        def _():
            convolve(i - look)

    @pl.loop(0, items)
    def _(j):
        @pl.when(active(j))
        def _():
            for d, side in enumerate(SIDES):
                @pl.when(has(*side))
                def _():
                    edge(d, j).wait_send()

    if early:
        @pl.when(first)
        def _():
            for v in range(early):
                for n in range(PIECES):
                    piece(v, n).wait_send()

    @pl.when(onward)
    def _():
        for n in range(max(videos - DEPTH, 0), videos):
            sent(n).wait_send()

    if ahead:
        @pl.when(later)
        def _():
            for copy in loans:
                copy.wait_send()
            for j in range(videos, items):
                finish(j).wait_recv()


def on_device(
    base_frames, section_noise, noise_levels, spatial_kernel, temporal_kernel, output_weight
):
    videos, frames, rows, cols, channels = base_frames.shape
    ahead = AHEAD if lax.axis_size("section") == 2 and videos > max(AHEAD, LOOK) + 1 else 0
    early = EARLY if lax.axis_size("section") > 1 and videos > EARLY + DEPTH + max(AHEAD, LOOK) else 0
    items = videos + ahead
    flat = (frames, rows * cols, channels)
    edges = (len(SIDES), items, frames * cols, channels)
    assert frames == rows and frames % CHUNK == 0 and MARGIN % cols == 0
    assert rows * cols > 2 * MARGIN and frames > 2
    result = pl.pallas_call(
        functools.partial(kernel, videos, ahead, early, frames, rows, cols, channels),
        out_shape=pltpu.VMEM((videos,) + flat, jnp.bfloat16),
        in_specs=[pl.BlockSpec(memory_space=pltpu.VMEM)] + [pl.BlockSpec(memory_space=pltpu.HBM)] * 5,
        out_specs=pl.BlockSpec(memory_space=pltpu.VMEM),
        scratch_shapes=[
            pltpu.VMEM((items,) + flat, jnp.bfloat16),
            pltpu.VMEM((items,) + flat, jnp.bfloat16),
            pltpu.VMEM((items,) + flat, jnp.bfloat16),
            pltpu.VMEM((1 + ahead, 13, channels, channels), jnp.bfloat16),
            pltpu.VMEM((1 + ahead, 2, 4 * channels, 2 * channels), jnp.bfloat16),
            pltpu.VMEM((1 + ahead, 8, channels), jnp.float32),
            pltpu.VMEM((16, channels), jnp.bfloat16),
            pltpu.VMEM((16, channels), jnp.bfloat16),
            pltpu.VMEM((items,) + flat, jnp.float32),
            pltpu.VMEM((items, frames + 2, rows + 2, cols, channels), jnp.float32),
            pltpu.VMEM(edges, jnp.bfloat16),
            pltpu.VMEM(edges, jnp.bfloat16),
            pltpu.VMEM((EARLY,) + flat, jnp.bfloat16),
            pltpu.SemaphoreType.DMA((videos,)),
            pltpu.SemaphoreType.DMA((videos,)),
            pltpu.SemaphoreType.DMA((3,)),
            pltpu.SemaphoreType.DMA((items,)),
            pltpu.SemaphoreType.DMA((items,)),
            pltpu.SemaphoreType.DMA((len(SIDES), items)),
            pltpu.SemaphoreType.DMA((len(SIDES), items)),
            pltpu.SemaphoreType.DMA((4 + videos,)),
            pltpu.SemaphoreType.DMA((4 + videos,)),
            pltpu.SemaphoreType.DMA((EARLY, PIECES)),
            pltpu.SemaphoreType.DMA((EARLY, PIECES)),
        ],
        compiler_params=pltpu.CompilerParams(
            collective_id=0, has_side_effects=True, vmem_limit_bytes=58 * 2**20
        ),
    )(
        noise_levels.reshape(1, 1),
        base_frames.reshape((videos,) + flat),
        section_noise.reshape((videos,) + flat),
        spatial_kernel[0],
        temporal_kernel[0],
        output_weight,
    )
    return result.reshape((1,) + base_frames.shape)


def solution(mesh):
    return jax.shard_map(
        on_device,
        mesh=mesh,
        in_specs=(
            P(None, "frames", "space", None, None),
            P("section", None, "frames", "space", None, None),
            P("section"),
            P("section", None, None, None),
            P("section", None, None, None),
            P("section", None, None),
        ),
        out_specs=P("section", None, "frames", "space", None, None),
        check_vma=False,
    )
```

```python
import functools

import jax
import jax.numpy as jnp
from jax import lax
from jax.experimental import pallas as pl
from jax.experimental.pallas import tpu as pltpu
from jax.sharding import PartitionSpec as P

MESH = pl.DeviceIdType.MESH
SIDES = (("frames", 1), ("frames", -1), ("space", 1), ("space", -1))
CHUNK = 4
DEPTH = 2
AHEAD = 2
LOOK = 1
EARLY = 1
MARGIN = 16
PIECES = 5


def kernel(
    videos, ahead, early, frames, rows, cols, channels,
    level_ref, base_hbm, noise_hbm, spatial_hbm, temporal_hbm, output_hbm, out_ref,
    noise, prior, result, weights, packed, levels, level_out, level_in,
    noisy_ref, middle, edge_out, edge_in, inner,
    noise_sem, base_sem, weight_sem, chain_send, chain_recv, edge_send, edge_recv,
    lend_send, lend_recv, piece_send, piece_recv,
):
    place = {axis: lax.axis_index(axis) for axis in ("section", "frames", "space")}
    count = {axis: lax.axis_size(axis) for axis in place}

    around = {
        (axis, step): jnp.clip(place[axis] + step, 0, count[axis] - 1)
        for axis in place
        for step in (1, -1)
    }
    exists = {
        (axis, step): place[axis] < count[axis] - 1 if step > 0 else place[axis] > 0
        for axis, step in around
    }

    def has(axis, step):
        return exists[axis, step]

    def peer(axis, step):
        return {axis: around[axis, step]}

    first = place["section"] == 0
    later = jnp.logical_not(first)
    onward = has("section", 1)
    items = videos + ahead
    lag = max(ahead, LOOK) + 1
    look = jnp.where(first, LOOK, 1)

    def special(v):
        return jnp.logical_and(v >= videos - lag, v < videos - lag + ahead) if ahead else False

    def active(j):
        if not ahead:
            return j < videos
        usual = jnp.logical_and(j < videos, jnp.logical_not(special(j)))
        return jnp.logical_or(usual, jnp.logical_and(first, j < items))

    def load_noise(v):
        return pltpu.make_async_copy(noise_hbm.at[v], noise.at[v], noise_sem.at[v])

    def load_base(v):
        return pltpu.make_async_copy(base_hbm.at[v], prior.at[v], base_sem.at[v])

    def turn(v):
        return v - ahead * (v >= videos - lag + ahead).astype(jnp.int32) if ahead else v

    def sent(n):
        return pltpu.make_async_remote_copy(
            src_ref=result.at[0], dst_ref=prior.at[0],
            send_sem=chain_send.at[n], recv_sem=chain_recv.at[n],
            device_id=peer("section", 1), device_id_type=MESH,
        )

    def pass_on(v):
        return pltpu.make_async_remote_copy(
            src_ref=result.at[v], dst_ref=prior.at[v],
            send_sem=chain_send.at[turn(v)], recv_sem=chain_recv.at[turn(v)],
            device_id=peer("section", 1), device_id_type=MESH,
        )

    def piece(v, n):
        core = pl.ds(MARGIN, rows * cols - 2 * MARGIN)
        part = (
            (pl.ds(1, frames - 2), core),
            (pl.ds(0, frames), pl.ds(0, MARGIN)),
            (pl.ds(0, frames), pl.ds(rows * cols - MARGIN, MARGIN)),
            (pl.ds(0, 1), core),
            (pl.ds(frames - 1, 1), core),
        )[n]
        source = inner if n == 0 else result
        return pltpu.make_async_remote_copy(
            src_ref=source.at[v, part[0], part[1]], dst_ref=prior.at[v, part[0], part[1]],
            send_sem=piece_send.at[v, n], recv_sem=piece_recv.at[v, n],
            device_id=peer("section", 1), device_id_type=MESH,
        )

    def finish(j):
        return pltpu.make_async_remote_copy(
            src_ref=result.at[j], dst_ref=out_ref.at[j - lag],
            send_sem=chain_send.at[j - ahead], recv_sem=chain_recv.at[j - ahead],
            device_id=peer("section", 1), device_id_type=MESH,
        )

    def edge(d, v):
        return pltpu.make_async_remote_copy(
            src_ref=edge_out.at[d, v], dst_ref=edge_in.at[d, v],
            send_sem=edge_send.at[d, v], recv_sem=edge_recv.at[d, v],
            device_id=peer(*SIDES[d]), device_id_type=MESH,
        )

    parts = ((spatial_hbm, 0, 9), (temporal_hbm, 9, 3), (output_hbm, 12, 1))
    weight_loads = [
        pltpu.make_async_copy(source, weights.at[0, pl.ds(at, size)], weight_sem.at[n])
        for n, (source, at, size) in enumerate(parts)
    ]
    loans = []
    if ahead:
        pairs = [(level_out, level_in)]
        pairs += [(source, weights.at[1, pl.ds(at, size)]) for source, at, size in parts]
        for v in range(videos - lag, videos - lag + ahead):
            pairs.append((noise_hbm.at[v], noise.at[v + lag]))
        loans = [
            pltpu.make_async_remote_copy(
                src_ref=source, dst_ref=target, send_sem=lend_send.at[n], recv_sem=lend_recv.at[n],
                device_id=peer("section", -1), device_id_type=MESH,
            )
            for n, (source, target) in enumerate(pairs)
        ]

    def passes(v):
        if not ahead:
            return onward
        return jnp.logical_and(onward, jnp.logical_and(v < videos, jnp.logical_not(special(v))))

    def sends(v):
        return jnp.logical_or(passes(v), v >= videos)

    neighbours = SIDES + (("section", 1), ("section", -1))
    barrier = pltpu.get_barrier_semaphore()
    for axis, step in neighbours:
        @pl.when(has(axis, step))
        def _():
            pl.semaphore_signal(barrier, inc=1, device_id=peer(axis, step), device_id_type=MESH)

    @pl.loop(0, videos)
    def _(v):
        @pl.when(active(v))
        def _():
            load_noise(v).start()

        @pl.when(first)
        def _():
            load_base(v).start()

    for copy in weight_loads:
        copy.start()

    for d, (axis, step) in enumerate(SIDES):
        @pl.when(jnp.logical_not(has(axis, -step)))
        def _():
            edge_in[d] = jnp.zeros(edge_in.shape[1:], edge_in.dtype)

    levels[0] = jnp.broadcast_to(level_ref[...].astype(jnp.float32), levels.shape[1:])
    level_out[...] = jnp.broadcast_to(level_ref[...], level_out.shape)

    def pack(number):
        packed[number] = jnp.zeros(packed.shape[1:], packed.dtype)
        for a in range(3):
            line = pl.ds(a * channels, channels)
            packed[number, 0, line, :channels] = weights[number, 3 * a + 1]
            packed[number, 0, line, channels:] = weights[number, 3 * a + 2]
            packed[number, 1, line, :channels] = weights[number, 3 * a]
        packed[number, 0, 3 * channels :, :channels] = weights[number, 9]
        packed[number, 1, channels : 2 * channels, channels:] = weights[number, 10]
        packed[number, 1, 3 * channels :, channels:] = weights[number, 11]

    def normalise(v, number):
        noisy = prior[v].astype(jnp.float32) + levels[number][0:1] * noise[v].astype(jnp.float32)
        noisy_ref[v] = noisy
        square = (noisy * noisy).reshape(-1, channels)
        high = square.astype(jnp.bfloat16)
        low = (square - high.astype(jnp.float32)).astype(jnp.bfloat16)
        total = jnp.dot(
            jnp.concatenate([high, low], axis=-1),
            jnp.ones((2 * channels, channels), jnp.bfloat16),
            preferred_element_type=jnp.float32,
        )
        power = total.reshape(noisy.shape) * (1.0 / channels)
        normalized = (noisy * lax.rsqrt(power + 1e-05)).astype(jnp.bfloat16)
        x = normalized.astype(jnp.float32).reshape(frames, rows, cols, channels)
        edge_out[0, v] = normalized[frames - 1]
        edge_out[1, v] = normalized[0]
        edge_out[2, v] = x[:, rows - 1].reshape(frames * cols, channels).astype(jnp.bfloat16)
        edge_out[3, v] = x[:, 0].reshape(frames * cols, channels).astype(jnp.bfloat16)
        middle[v, 1 : 1 + frames, 1 : 1 + rows] = x

    def send_edges(v):
        for d, side in enumerate(SIDES):
            @pl.when(has(*side))
            def _():
                edge(d, v).start()

    def prepare(i):
        @pl.when(i < videos)
        def _():
            load_noise(i).wait()

            @pl.when(first)
            def _():
                load_base(i).wait()

            if early:
                second = place["section"] == 1
                for v in range(early):
                    @pl.when(jnp.logical_and(second, i == v))
                    def _():
                        for n in range(PIECES):
                            piece(v, n).wait_recv()

                whole = jnp.logical_or(place["section"] > 1, jnp.logical_and(second, i >= early))
            else:
                whole = later

            @pl.when(whole)
            def _():
                pass_on(i).wait_recv()

        if ahead:
            @pl.when(i == videos)
            def _():
                for copy in loans:
                    copy.wait_recv()
                levels[1] = level_in[0:8].astype(jnp.float32)
                pack(1)

            @pl.when(i >= videos)
            def _():
                prior[i] = result[i - lag]

        normalise(i, (i >= videos).astype(jnp.int32) if ahead else 0)

    def estimate_into(target, v, number):
        projection = weights[number, 12]
        level = levels[number][0:1]
        lines = CHUNK * rows
        column = lax.broadcasted_iota(jnp.int32, (lines, cols, channels), 1)
        for f in range(0, frames, CHUNK):
            views = [middle[v, f + 1 : f + 1 + CHUNK, a : a + rows] for a in range(3)]
            views += [middle[v, f + t : f + t + CHUNK, 1 : 1 + rows] for t in (0, 2)]
            views = [view.reshape(-1, channels).astype(jnp.bfloat16) for view in views]
            sums = [
                jnp.dot(
                    jnp.concatenate(views[:3] + [views[3 + n]], axis=-1), packed[number, n],
                    preferred_element_type=jnp.float32,
                )
                for n in range(2)
            ]
            ahead_part = sums[0][:, channels:].reshape(lines, cols, channels)
            behind_part = sums[1][:, :channels].reshape(lines, cols, channels)
            shifted = jnp.where(column == cols - 1, 0.0, pltpu.roll(ahead_part, cols - 1, 1))
            shifted = shifted + jnp.where(column == 0, 0.0, pltpu.roll(behind_part, 1, 1))
            pre = sums[0][:, :channels] + sums[1][:, channels:] + shifted.reshape(-1, channels)
            activated = (0.5 * pre * (1.0 + jnp.tanh(0.5 * pre))).astype(jnp.bfloat16)
            estimate = jnp.dot(activated, projection, preferred_element_type=jnp.float32)
            held = noisy_ref[v, f : f + CHUNK]
            target[v, f : f + CHUNK] = (held - level * estimate.reshape(held.shape)).astype(
                jnp.bfloat16
            )

    def convolve(v):
        for d, (axis, step) in enumerate(SIDES):
            @pl.when(has(axis, -step))
            def _():
                edge(d, v).wait_recv()
        number = (v >= videos).astype(jnp.int32) if ahead else 0
        middle[v, 0, 1 : 1 + rows] = edge_in[0, v].astype(jnp.float32).reshape(rows, cols, channels)
        middle[v, frames + 1, 1 : 1 + rows] = (
            edge_in[1, v].astype(jnp.float32).reshape(rows, cols, channels)
        )
        for d, at in ((2, 0), (3, rows + 1)):
            middle[v, 1 : 1 + frames, at] = (
                edge_in[d, v].astype(jnp.float32).reshape(frames, cols, channels)
            )
        estimate_into(result, v, number)

        wholes = jnp.where(first, early, 0)

        @pl.when(jnp.logical_and(turn(v) >= DEPTH + wholes, sends(v)))
        def _():
            sent(turn(v) - DEPTH).wait_send()

        for w in range(early):
            @pl.when(jnp.logical_and(first, v == w))
            def _():
                for n in range(1, PIECES):
                    piece(w, n).start()

        @pl.when(jnp.logical_and(passes(v), v >= wholes))
        def _():
            pass_on(v).start()

        if ahead:
            @pl.when(v >= videos)
            def _():
                finish(v).start()

        @pl.when(v < videos)
        def _():
            out_ref[v] = result[v]

    for copy in weight_loads:
        copy.wait()
    pack(0)

    def start(v):
        load_noise(v).wait()
        load_base(v).wait()
        normalise(v, 0)

    @pl.when(first)
    def _():
        start(0)
        if early:
            estimate_into(inner, 0, 0)

    pl.semaphore_wait(barrier, sum(has(*side).astype(jnp.int32) for side in neighbours))

    @pl.when(first)
    def _():
        send_edges(0)
        if early:
            piece(0, 0).start()
        for v in range(1, early):
            start(v)
            send_edges(v)
            estimate_into(inner, v, 0)
            piece(v, 0).start()

    if ahead:
        @pl.when(later)
        def _():
            for copy in loans:
                copy.start()

    @pl.loop(0, items + LOOK)
    def _(i):
        @pl.when(jnp.logical_and(active(i), jnp.logical_or(i >= max(early, 1), later)))
        def _():
            prepare(i)
            send_edges(i)

        @pl.when(jnp.logical_and(i >= look, active(i - look)))
        def _():
            convolve(i - look)

    @pl.loop(0, items)
    def _(j):
        @pl.when(active(j))
        def _():
            for d, side in enumerate(SIDES):
                @pl.when(has(*side))
                def _():
                    edge(d, j).wait_send()

    if early:
        @pl.when(first)
        def _():
            for v in range(early):
                for n in range(PIECES):
                    piece(v, n).wait_send()

    @pl.when(onward)
    def _():
        for n in range(max(videos - DEPTH, 0), videos):
            sent(n).wait_send()

    if ahead:
        @pl.when(later)
        def _():
            for copy in loans:
                copy.wait_send()
            for j in range(videos, items):
                finish(j).wait_recv()


def on_device(
    base_frames, section_noise, noise_levels, spatial_kernel, temporal_kernel, output_weight
):
    videos, frames, rows, cols, channels = base_frames.shape
    ahead = AHEAD if lax.axis_size("section") == 2 and videos > max(AHEAD, LOOK) + 1 else 0
    early = EARLY if lax.axis_size("section") > 1 and videos > EARLY + DEPTH + max(AHEAD, LOOK) else 0
    items = videos + ahead
    flat = (frames, rows * cols, channels)
    edges = (len(SIDES), items, frames * cols, channels)
    assert frames == rows and frames % CHUNK == 0 and MARGIN % cols == 0
    assert rows * cols > 2 * MARGIN and frames > 2
    result = pl.pallas_call(
        functools.partial(kernel, videos, ahead, early, frames, rows, cols, channels),
        out_shape=pltpu.VMEM((videos,) + flat, jnp.bfloat16),
        in_specs=[pl.BlockSpec(memory_space=pltpu.VMEM)] + [pl.BlockSpec(memory_space=pltpu.HBM)] * 5,
        out_specs=pl.BlockSpec(memory_space=pltpu.VMEM),
        scratch_shapes=[
            pltpu.VMEM((items,) + flat, jnp.bfloat16),
            pltpu.VMEM((items,) + flat, jnp.bfloat16),
            pltpu.VMEM((items,) + flat, jnp.bfloat16),
            pltpu.VMEM((1 + ahead, 13, channels, channels), jnp.bfloat16),
            pltpu.VMEM((1 + ahead, 2, 4 * channels, 2 * channels), jnp.bfloat16),
            pltpu.VMEM((1 + ahead, 8, channels), jnp.float32),
            pltpu.VMEM((16, channels), jnp.bfloat16),
            pltpu.VMEM((16, channels), jnp.bfloat16),
            pltpu.VMEM((items,) + flat, jnp.float32),
            pltpu.VMEM((items, frames + 2, rows + 2, cols, channels), jnp.float32),
            pltpu.VMEM(edges, jnp.bfloat16),
            pltpu.VMEM(edges, jnp.bfloat16),
            pltpu.VMEM((EARLY,) + flat, jnp.bfloat16),
            pltpu.SemaphoreType.DMA((videos,)),
            pltpu.SemaphoreType.DMA((videos,)),
            pltpu.SemaphoreType.DMA((3,)),
            pltpu.SemaphoreType.DMA((items,)),
            pltpu.SemaphoreType.DMA((items,)),
            pltpu.SemaphoreType.DMA((len(SIDES), items)),
            pltpu.SemaphoreType.DMA((len(SIDES), items)),
            pltpu.SemaphoreType.DMA((4 + videos,)),
            pltpu.SemaphoreType.DMA((4 + videos,)),
            pltpu.SemaphoreType.DMA((EARLY, PIECES)),
            pltpu.SemaphoreType.DMA((EARLY, PIECES)),
        ],
        compiler_params=pltpu.CompilerParams(
            collective_id=0, has_side_effects=True, vmem_limit_bytes=58 * 2**20
        ),
    )(
        noise_levels.reshape(1, 1),
        base_frames.reshape((videos,) + flat),
        section_noise.reshape((videos,) + flat),
        spatial_kernel[0],
        temporal_kernel[0],
        output_weight,
    )
    return result.reshape((1,) + base_frames.shape)


def solution(mesh):
    return jax.shard_map(
        on_device,
        mesh=mesh,
        in_specs=(
            P(None, "frames", "space", None, None),
            P("section", None, "frames", "space", None, None),
            P("section"),
            P("section", None, None, None),
            P("section", None, None, None),
            P("section", None, None),
        ),
        out_specs=P("section", None, "frames", "space", None, None),
        check_vma=False,
    )
```

```python
import functools

import jax
import jax.numpy as jnp
from jax import lax
from jax.experimental import pallas as pl
from jax.experimental.pallas import tpu as pltpu
from jax.sharding import PartitionSpec as P

MESH = pl.DeviceIdType.MESH
SIDES = (("frames", 1), ("frames", -1), ("space", 1), ("space", -1))
CHUNK = 8
DEPTH = 2
AHEAD = 2
EARLY = 1
MARGIN = 16
PIECES = 5


def kernel(
    videos, ahead, early, frames, rows, cols, channels,
    level_ref, base_hbm, noise_hbm, spatial_hbm, temporal_hbm, output_hbm, out_ref,
    noise, prior, result, weights, packed, levels, level_out, level_in,
    noisy_ref, middle, edge_out, edge_in, inner,
    noise_sem, base_sem, weight_sem, chain_send, chain_recv, edge_send, edge_recv,
    lend_send, lend_recv, piece_send, piece_recv,
):
    place = {axis: lax.axis_index(axis) for axis in ("section", "frames", "space")}
    count = {axis: lax.axis_size(axis) for axis in place}

    around = {
        (axis, step): jnp.clip(place[axis] + step, 0, count[axis] - 1)
        for axis in place
        for step in (1, -1)
    }
    exists = {
        (axis, step): place[axis] < count[axis] - 1 if step > 0 else place[axis] > 0
        for axis, step in around
    }

    def has(axis, step):
        return exists[axis, step]

    def peer(axis, step):
        return {axis: around[axis, step]}

    first = place["section"] == 0
    later = jnp.logical_not(first)
    onward = has("section", 1)
    items = videos + ahead
    lag = ahead + 1

    def special(v):
        return jnp.logical_and(v >= videos - lag, v < videos - 1) if ahead else False

    def active(j):
        if not ahead:
            return j < videos
        usual = jnp.logical_and(j < videos, jnp.logical_not(special(j)))
        return jnp.logical_or(usual, jnp.logical_and(first, j < items))

    def load_noise(v):
        return pltpu.make_async_copy(noise_hbm.at[v], noise.at[v], noise_sem.at[v])

    def load_base(v):
        return pltpu.make_async_copy(base_hbm.at[v], prior.at[v], base_sem.at[v])

    def turn(v):
        return v - ahead * (v >= videos - 1).astype(jnp.int32) if ahead else v

    def sent(n):
        return pltpu.make_async_remote_copy(
            src_ref=result.at[0], dst_ref=prior.at[0],
            send_sem=chain_send.at[n], recv_sem=chain_recv.at[n],
            device_id=peer("section", 1), device_id_type=MESH,
        )

    def pass_on(v):
        return pltpu.make_async_remote_copy(
            src_ref=result.at[v], dst_ref=prior.at[v],
            send_sem=chain_send.at[turn(v)], recv_sem=chain_recv.at[turn(v)],
            device_id=peer("section", 1), device_id_type=MESH,
        )

    def piece(v, n):
        core = pl.ds(MARGIN, rows * cols - 2 * MARGIN)
        part = (
            (pl.ds(1, frames - 2), core),
            (pl.ds(0, frames), pl.ds(0, MARGIN)),
            (pl.ds(0, frames), pl.ds(rows * cols - MARGIN, MARGIN)),
            (pl.ds(0, 1), core),
            (pl.ds(frames - 1, 1), core),
        )[n]
        source = inner if n == 0 else result
        return pltpu.make_async_remote_copy(
            src_ref=source.at[v, part[0], part[1]], dst_ref=prior.at[v, part[0], part[1]],
            send_sem=piece_send.at[v, n], recv_sem=piece_recv.at[v, n],
            device_id=peer("section", 1), device_id_type=MESH,
        )

    def finish(j):
        return pltpu.make_async_remote_copy(
            src_ref=result.at[j], dst_ref=out_ref.at[j - lag],
            send_sem=chain_send.at[j - ahead], recv_sem=chain_recv.at[j - ahead],
            device_id=peer("section", 1), device_id_type=MESH,
        )

    def edge(d, v):
        return pltpu.make_async_remote_copy(
            src_ref=edge_out.at[d, v], dst_ref=edge_in.at[d, v],
            send_sem=edge_send.at[d, v], recv_sem=edge_recv.at[d, v],
            device_id=peer(*SIDES[d]), device_id_type=MESH,
        )

    parts = ((spatial_hbm, 0, 9), (temporal_hbm, 9, 3), (output_hbm, 12, 1))
    weight_loads = [
        pltpu.make_async_copy(source, weights.at[0, pl.ds(at, size)], weight_sem.at[n])
        for n, (source, at, size) in enumerate(parts)
    ]
    loans = []
    if ahead:
        pairs = [(level_out, level_in)]
        pairs += [(source, weights.at[1, pl.ds(at, size)]) for source, at, size in parts]
        for v in range(videos - lag, videos - 1):
            pairs.append((noise_hbm.at[v], noise.at[v + lag]))
        loans = [
            pltpu.make_async_remote_copy(
                src_ref=source, dst_ref=target, send_sem=lend_send.at[n], recv_sem=lend_recv.at[n],
                device_id=peer("section", -1), device_id_type=MESH,
            )
            for n, (source, target) in enumerate(pairs)
        ]

    def passes(v):
        if not ahead:
            return onward
        return jnp.logical_and(onward, jnp.logical_and(v < videos, jnp.logical_not(special(v))))

    def sends(v):
        return jnp.logical_or(passes(v), v >= videos)

    neighbours = SIDES + (("section", 1), ("section", -1))
    barrier = pltpu.get_barrier_semaphore()
    for axis, step in neighbours:
        @pl.when(has(axis, step))
        def _():
            pl.semaphore_signal(barrier, inc=1, device_id=peer(axis, step), device_id_type=MESH)

    @pl.loop(0, videos)
    def _(v):
        @pl.when(active(v))
        def _():
            load_noise(v).start()

        @pl.when(first)
        def _():
            load_base(v).start()

    for copy in weight_loads:
        copy.start()

    for d, (axis, step) in enumerate(SIDES):
        @pl.when(jnp.logical_not(has(axis, -step)))
        def _():
            edge_in[d] = jnp.zeros(edge_in.shape[1:], edge_in.dtype)

    levels[0] = jnp.broadcast_to(level_ref[...].astype(jnp.float32), levels.shape[1:])
    level_out[...] = jnp.broadcast_to(level_ref[...], level_out.shape)

    def pack(number):
        packed[number] = jnp.zeros(packed.shape[1:], packed.dtype)
        for a in range(3):
            line = pl.ds(a * channels, channels)
            packed[number, 0, line, :channels] = weights[number, 3 * a + 1]
            packed[number, 0, line, channels:] = weights[number, 3 * a + 2]
            packed[number, 1, line, :channels] = weights[number, 3 * a]
        packed[number, 0, 3 * channels :, :channels] = weights[number, 9]
        packed[number, 1, channels : 2 * channels, channels:] = weights[number, 10]
        packed[number, 1, 3 * channels :, channels:] = weights[number, 11]

    def normalise(v, number):
        noisy = prior[v].astype(jnp.float32) + levels[number][0:1] * noise[v].astype(jnp.float32)
        noisy_ref[v] = noisy
        power = jnp.mean(noisy * noisy, axis=-1, keepdims=True)
        normalized = (noisy * lax.rsqrt(power + 1e-05)).astype(jnp.bfloat16)
        x = normalized.astype(jnp.float32).reshape(frames, rows, cols, channels)
        edge_out[0, v] = normalized[frames - 1]
        edge_out[1, v] = normalized[0]
        edge_out[2, v] = x[:, rows - 1].reshape(frames * cols, channels).astype(jnp.bfloat16)
        edge_out[3, v] = x[:, 0].reshape(frames * cols, channels).astype(jnp.bfloat16)
        middle[v, 1 : 1 + frames, 1 : 1 + rows] = x

    def send_edges(v):
        for d, side in enumerate(SIDES):
            @pl.when(has(*side))
            def _():
                edge(d, v).start()

    def prepare(i):
        @pl.when(i < videos)
        def _():
            load_noise(i).wait()

            @pl.when(first)
            def _():
                load_base(i).wait()

            if early:
                second = place["section"] == 1
                for v in range(early):
                    @pl.when(jnp.logical_and(second, i == v))
                    def _():
                        for n in range(PIECES):
                            piece(v, n).wait_recv()

                whole = jnp.logical_or(place["section"] > 1, jnp.logical_and(second, i >= early))
            else:
                whole = later

            @pl.when(whole)
            def _():
                pass_on(i).wait_recv()

        if ahead:
            @pl.when(i == videos)
            def _():
                for copy in loans:
                    copy.wait_recv()
                levels[1] = level_in[0:8].astype(jnp.float32)
                pack(1)

            @pl.when(i >= videos)
            def _():
                prior[i] = result[i - lag]

        normalise(i, (i >= videos).astype(jnp.int32) if ahead else 0)

    def estimate_into(target, v, number):
        projection = weights[number, 12]
        level = levels[number][0:1]
        lines = CHUNK * rows
        column = lax.broadcasted_iota(jnp.int32, (lines, cols, channels), 1)
        for f in range(0, frames, CHUNK):
            views = [middle[v, f + 1 : f + 1 + CHUNK, a : a + rows] for a in range(3)]
            views += [middle[v, f + t : f + t + CHUNK, 1 : 1 + rows] for t in (0, 2)]
            views = [view.reshape(-1, channels).astype(jnp.bfloat16) for view in views]
            sums = [
                jnp.dot(
                    jnp.concatenate(views[:3] + [views[3 + n]], axis=-1), packed[number, n],
                    preferred_element_type=jnp.float32,
                )
                for n in range(2)
            ]
            ahead_part = sums[0][:, channels:].reshape(lines, cols, channels)
            behind_part = sums[1][:, :channels].reshape(lines, cols, channels)
            shifted = jnp.where(column == cols - 1, 0.0, pltpu.roll(ahead_part, cols - 1, 1))
            shifted = shifted + jnp.where(column == 0, 0.0, pltpu.roll(behind_part, 1, 1))
            pre = sums[0][:, :channels] + sums[1][:, channels:] + shifted.reshape(-1, channels)
            activated = (0.5 * pre * (1.0 + jnp.tanh(0.5 * pre))).astype(jnp.bfloat16)
            estimate = jnp.dot(activated, projection, preferred_element_type=jnp.float32)
            held = noisy_ref[v, f : f + CHUNK]
            target[v, f : f + CHUNK] = (held - level * estimate.reshape(held.shape)).astype(
                jnp.bfloat16
            )

    def convolve(v):
        for d, (axis, step) in enumerate(SIDES):
            @pl.when(has(axis, -step))
            def _():
                edge(d, v).wait_recv()
        number = (v >= videos).astype(jnp.int32) if ahead else 0
        middle[v, 0, 1 : 1 + rows] = edge_in[0, v].astype(jnp.float32).reshape(rows, cols, channels)
        middle[v, frames + 1, 1 : 1 + rows] = (
            edge_in[1, v].astype(jnp.float32).reshape(rows, cols, channels)
        )
        for d, at in ((2, 0), (3, rows + 1)):
            middle[v, 1 : 1 + frames, at] = (
                edge_in[d, v].astype(jnp.float32).reshape(frames, cols, channels)
            )
        estimate_into(result, v, number)

        wholes = jnp.where(first, early, 0)

        @pl.when(jnp.logical_and(turn(v) >= DEPTH + wholes, sends(v)))
        def _():
            sent(turn(v) - DEPTH).wait_send()

        for w in range(early):
            @pl.when(jnp.logical_and(first, v == w))
            def _():
                for n in range(1, PIECES):
                    piece(w, n).start()

        @pl.when(jnp.logical_and(passes(v), v >= wholes))
        def _():
            pass_on(v).start()

        if ahead:
            @pl.when(v >= videos)
            def _():
                finish(v).start()

        @pl.when(v < videos)
        def _():
            out_ref[v] = result[v]

    for copy in weight_loads:
        copy.wait()
    pack(0)

    def start(v):
        load_noise(v).wait()
        load_base(v).wait()
        normalise(v, 0)

    @pl.when(first)
    def _():
        start(0)
        if early:
            estimate_into(inner, 0, 0)

    pl.semaphore_wait(barrier, sum(has(*side).astype(jnp.int32) for side in neighbours))

    @pl.when(first)
    def _():
        send_edges(0)
        if early:
            piece(0, 0).start()
        for v in range(1, early):
            start(v)
            send_edges(v)
            estimate_into(inner, v, 0)
            piece(v, 0).start()

    if ahead:
        @pl.when(later)
        def _():
            for copy in loans:
                copy.start()

    @pl.loop(0, items + 1)
    def _(i):
        @pl.when(jnp.logical_and(active(i), jnp.logical_or(i >= max(early, 1), later)))
        def _():
            prepare(i)
            send_edges(i)

        @pl.when(jnp.logical_and(i > 0, active(i - 1)))
        def _():
            convolve(i - 1)

    @pl.loop(0, items)
    def _(j):
        @pl.when(active(j))
        def _():
            for d, side in enumerate(SIDES):
                @pl.when(has(*side))
                def _():
                    edge(d, j).wait_send()

    if early:
        @pl.when(first)
        def _():
            for v in range(early):
                for n in range(PIECES):
                    piece(v, n).wait_send()

    @pl.when(onward)
    def _():
        for n in range(max(videos - DEPTH, 0), videos):
            sent(n).wait_send()

    if ahead:
        @pl.when(later)
        def _():
            for copy in loans:
                copy.wait_send()
            for j in range(videos, items):
                finish(j).wait_recv()


def on_device(
    base_frames, section_noise, noise_levels, spatial_kernel, temporal_kernel, output_weight
):
    videos, frames, rows, cols, channels = base_frames.shape
    ahead = AHEAD if lax.axis_size("section") == 2 and videos > AHEAD + 1 else 0
    early = EARLY if lax.axis_size("section") > 1 and videos >= EARLY + DEPTH + ahead else 0
    items = videos + ahead
    flat = (frames, rows * cols, channels)
    edges = (len(SIDES), items, frames * cols, channels)
    assert frames == rows and frames % CHUNK == 0 and MARGIN % cols == 0
    assert rows * cols > 2 * MARGIN and frames > 2
    result = pl.pallas_call(
        functools.partial(kernel, videos, ahead, early, frames, rows, cols, channels),
        out_shape=pltpu.VMEM((videos,) + flat, jnp.bfloat16),
        in_specs=[pl.BlockSpec(memory_space=pltpu.VMEM)] + [pl.BlockSpec(memory_space=pltpu.HBM)] * 5,
        out_specs=pl.BlockSpec(memory_space=pltpu.VMEM),
        scratch_shapes=[
            pltpu.VMEM((items,) + flat, jnp.bfloat16),
            pltpu.VMEM((items,) + flat, jnp.bfloat16),
            pltpu.VMEM((items,) + flat, jnp.bfloat16),
            pltpu.VMEM((1 + ahead, 13, channels, channels), jnp.bfloat16),
            pltpu.VMEM((1 + ahead, 2, 4 * channels, 2 * channels), jnp.bfloat16),
            pltpu.VMEM((1 + ahead, 8, channels), jnp.float32),
            pltpu.VMEM((16, channels), jnp.bfloat16),
            pltpu.VMEM((16, channels), jnp.bfloat16),
            pltpu.VMEM((items,) + flat, jnp.float32),
            pltpu.VMEM((items, frames + 2, rows + 2, cols, channels), jnp.float32),
            pltpu.VMEM(edges, jnp.bfloat16),
            pltpu.VMEM(edges, jnp.bfloat16),
            pltpu.VMEM((EARLY,) + flat, jnp.bfloat16),
            pltpu.SemaphoreType.DMA((videos,)),
            pltpu.SemaphoreType.DMA((videos,)),
            pltpu.SemaphoreType.DMA((3,)),
            pltpu.SemaphoreType.DMA((items,)),
            pltpu.SemaphoreType.DMA((items,)),
            pltpu.SemaphoreType.DMA((len(SIDES), items)),
            pltpu.SemaphoreType.DMA((len(SIDES), items)),
            pltpu.SemaphoreType.DMA((4 + videos,)),
            pltpu.SemaphoreType.DMA((4 + videos,)),
            pltpu.SemaphoreType.DMA((EARLY, PIECES)),
            pltpu.SemaphoreType.DMA((EARLY, PIECES)),
        ],
        compiler_params=pltpu.CompilerParams(
            collective_id=0, has_side_effects=True, vmem_limit_bytes=58 * 2**20
        ),
    )(
        noise_levels.reshape(1, 1),
        base_frames.reshape((videos,) + flat),
        section_noise.reshape((videos,) + flat),
        spatial_kernel[0],
        temporal_kernel[0],
        output_weight,
    )
    return result.reshape((1,) + base_frames.shape)


def solution(mesh):
    return jax.shard_map(
        on_device,
        mesh=mesh,
        in_specs=(
            P(None, "frames", "space", None, None),
            P("section", None, "frames", "space", None, None),
            P("section"),
            P("section", None, None, None),
            P("section", None, None, None),
            P("section", None, None),
        ),
        out_specs=P("section", None, "frames", "space", None, None),
        check_vma=False,
    )
```

```python
import functools

import jax
import jax.numpy as jnp
from jax import lax
from jax.experimental import pallas as pl
from jax.experimental.pallas import tpu as pltpu
from jax.sharding import PartitionSpec as P

MESH = pl.DeviceIdType.MESH
SIDES = (("frames", 1), ("frames", -1), ("space", 1), ("space", -1))
CHUNK = 8
DEPTH = 2
AHEAD = 1
EARLY = 1
MARGIN = 16
PIECES = 5


def kernel(
    videos, ahead, early, frames, rows, cols, channels,
    level_ref, base_hbm, noise_hbm, spatial_hbm, temporal_hbm, output_hbm, out_ref,
    noise, prior, result, weights, packed, levels, level_out, level_in,
    noisy_ref, middle, edge_out, edge_in, inner,
    noise_sem, base_sem, weight_sem, chain_send, chain_recv, edge_send, edge_recv,
    lend_send, lend_recv, piece_send, piece_recv,
):
    place = {axis: lax.axis_index(axis) for axis in ("section", "frames", "space")}
    count = {axis: lax.axis_size(axis) for axis in place}

    around = {
        (axis, step): jnp.clip(place[axis] + step, 0, count[axis] - 1)
        for axis in place
        for step in (1, -1)
    }
    exists = {
        (axis, step): place[axis] < count[axis] - 1 if step > 0 else place[axis] > 0
        for axis, step in around
    }

    def has(axis, step):
        return exists[axis, step]

    def peer(axis, step):
        return {axis: around[axis, step]}

    first = place["section"] == 0
    later = jnp.logical_not(first)
    onward = has("section", 1)
    items = videos + ahead
    lag = ahead + 1

    def special(v):
        return jnp.logical_and(v >= videos - lag, v < videos - 1) if ahead else False

    def active(j):
        if not ahead:
            return j < videos
        usual = jnp.logical_and(j < videos, jnp.logical_not(special(j)))
        return jnp.logical_or(usual, jnp.logical_and(first, j < items))

    def load_noise(v):
        return pltpu.make_async_copy(noise_hbm.at[v], noise.at[v], noise_sem.at[v])

    def load_base(v):
        return pltpu.make_async_copy(base_hbm.at[v], prior.at[v], base_sem.at[v])

    def turn(v):
        return v - ahead * (v >= videos - 1).astype(jnp.int32) if ahead else v

    def sent(n):
        return pltpu.make_async_remote_copy(
            src_ref=result.at[0], dst_ref=prior.at[0],
            send_sem=chain_send.at[n], recv_sem=chain_recv.at[n],
            device_id=peer("section", 1), device_id_type=MESH,
        )

    def pass_on(v):
        return pltpu.make_async_remote_copy(
            src_ref=result.at[v], dst_ref=prior.at[v],
            send_sem=chain_send.at[turn(v)], recv_sem=chain_recv.at[turn(v)],
            device_id=peer("section", 1), device_id_type=MESH,
        )

    def piece(v, n):
        core = pl.ds(MARGIN, rows * cols - 2 * MARGIN)
        part = (
            (pl.ds(1, frames - 2), core),
            (pl.ds(0, frames), pl.ds(0, MARGIN)),
            (pl.ds(0, frames), pl.ds(rows * cols - MARGIN, MARGIN)),
            (pl.ds(0, 1), core),
            (pl.ds(frames - 1, 1), core),
        )[n]
        source = inner if n == 0 else result
        return pltpu.make_async_remote_copy(
            src_ref=source.at[v, part[0], part[1]], dst_ref=prior.at[v, part[0], part[1]],
            send_sem=piece_send.at[v, n], recv_sem=piece_recv.at[v, n],
            device_id=peer("section", 1), device_id_type=MESH,
        )

    def finish(j):
        return pltpu.make_async_remote_copy(
            src_ref=result.at[j], dst_ref=out_ref.at[j - lag],
            send_sem=chain_send.at[j - ahead], recv_sem=chain_recv.at[j - ahead],
            device_id=peer("section", 1), device_id_type=MESH,
        )

    def edge(d, v):
        return pltpu.make_async_remote_copy(
            src_ref=edge_out.at[d, v], dst_ref=edge_in.at[d, v],
            send_sem=edge_send.at[d, v], recv_sem=edge_recv.at[d, v],
            device_id=peer(*SIDES[d]), device_id_type=MESH,
        )

    parts = ((spatial_hbm, 0, 9), (temporal_hbm, 9, 3), (output_hbm, 12, 1))
    weight_loads = [
        pltpu.make_async_copy(source, weights.at[0, pl.ds(at, size)], weight_sem.at[n])
        for n, (source, at, size) in enumerate(parts)
    ]
    loans = []
    if ahead:
        pairs = [(level_out, level_in)]
        pairs += [(source, weights.at[1, pl.ds(at, size)]) for source, at, size in parts]
        for v in range(videos - lag, videos - 1):
            pairs.append((noise_hbm.at[v], noise.at[v + lag]))
        loans = [
            pltpu.make_async_remote_copy(
                src_ref=source, dst_ref=target, send_sem=lend_send.at[n], recv_sem=lend_recv.at[n],
                device_id=peer("section", -1), device_id_type=MESH,
            )
            for n, (source, target) in enumerate(pairs)
        ]

    def passes(v):
        if not ahead:
            return onward
        return jnp.logical_and(onward, jnp.logical_and(v < videos, jnp.logical_not(special(v))))

    def sends(v):
        return jnp.logical_or(passes(v), v >= videos)

    neighbours = SIDES + (("section", 1), ("section", -1))
    barrier = pltpu.get_barrier_semaphore()
    for axis, step in neighbours:
        @pl.when(has(axis, step))
        def _():
            pl.semaphore_signal(barrier, inc=1, device_id=peer(axis, step), device_id_type=MESH)

    @pl.loop(0, videos)
    def _(v):
        @pl.when(active(v))
        def _():
            load_noise(v).start()

        @pl.when(first)
        def _():
            load_base(v).start()

    for copy in weight_loads:
        copy.start()

    for d, (axis, step) in enumerate(SIDES):
        @pl.when(jnp.logical_not(has(axis, -step)))
        def _():
            edge_in[d] = jnp.zeros(edge_in.shape[1:], edge_in.dtype)

    levels[0] = jnp.broadcast_to(level_ref[...].astype(jnp.float32), levels.shape[1:])
    level_out[...] = jnp.broadcast_to(level_ref[...], level_out.shape)

    def pack(number):
        packed[number] = jnp.zeros(packed.shape[1:], packed.dtype)
        for a in range(3):
            line = pl.ds(a * channels, channels)
            packed[number, 0, line, :channels] = weights[number, 3 * a + 1]
            packed[number, 0, line, channels:] = weights[number, 3 * a + 2]
            packed[number, 1, line, :channels] = weights[number, 3 * a]
        packed[number, 0, 3 * channels :, :channels] = weights[number, 9]
        packed[number, 1, channels : 2 * channels, channels:] = weights[number, 10]
        packed[number, 1, 3 * channels :, channels:] = weights[number, 11]

    def normalise(v, number):
        noisy = prior[v].astype(jnp.float32) + levels[number][0:1] * noise[v].astype(jnp.float32)
        noisy_ref[v] = noisy
        power = jnp.mean(noisy * noisy, axis=-1, keepdims=True)
        normalized = (noisy * lax.rsqrt(power + 1e-05)).astype(jnp.bfloat16)
        x = normalized.astype(jnp.float32).reshape(frames, rows, cols, channels)
        edge_out[0, v] = normalized[frames - 1]
        edge_out[1, v] = normalized[0]
        edge_out[2, v] = x[:, rows - 1].reshape(frames * cols, channels).astype(jnp.bfloat16)
        edge_out[3, v] = x[:, 0].reshape(frames * cols, channels).astype(jnp.bfloat16)
        middle[v, 1 : 1 + frames, 1 : 1 + rows] = x

    def send_edges(v):
        for d, side in enumerate(SIDES):
            @pl.when(has(*side))
            def _():
                edge(d, v).start()

    def prepare(i):
        @pl.when(i < videos)
        def _():
            load_noise(i).wait()

            @pl.when(first)
            def _():
                load_base(i).wait()

            if early:
                second = place["section"] == 1
                for v in range(early):
                    @pl.when(jnp.logical_and(second, i == v))
                    def _():
                        for n in range(PIECES):
                            piece(v, n).wait_recv()

                whole = jnp.logical_or(place["section"] > 1, jnp.logical_and(second, i >= early))
            else:
                whole = later

            @pl.when(whole)
            def _():
                pass_on(i).wait_recv()

        if ahead:
            @pl.when(i == videos)
            def _():
                for copy in loans:
                    copy.wait_recv()
                levels[1] = level_in[0:8].astype(jnp.float32)
                pack(1)

            @pl.when(i >= videos)
            def _():
                prior[i] = result[i - lag]

        normalise(i, (i >= videos).astype(jnp.int32) if ahead else 0)

    def estimate_into(target, v, number):
        projection = weights[number, 12]
        level = levels[number][0:1]
        lines = CHUNK * rows
        column = lax.broadcasted_iota(jnp.int32, (lines, cols, channels), 1)
        for f in range(0, frames, CHUNK):
            views = [middle[v, f + 1 : f + 1 + CHUNK, a : a + rows] for a in range(3)]
            views += [middle[v, f + t : f + t + CHUNK, 1 : 1 + rows] for t in (0, 2)]
            views = [view.reshape(-1, channels).astype(jnp.bfloat16) for view in views]
            sums = [
                jnp.dot(
                    jnp.concatenate(views[:3] + [views[3 + n]], axis=-1), packed[number, n],
                    preferred_element_type=jnp.float32,
                )
                for n in range(2)
            ]
            ahead_part = sums[0][:, channels:].reshape(lines, cols, channels)
            behind_part = sums[1][:, :channels].reshape(lines, cols, channels)
            shifted = jnp.where(column == cols - 1, 0.0, pltpu.roll(ahead_part, cols - 1, 1))
            shifted = shifted + jnp.where(column == 0, 0.0, pltpu.roll(behind_part, 1, 1))
            pre = sums[0][:, :channels] + sums[1][:, channels:] + shifted.reshape(-1, channels)
            activated = (0.5 * pre * (1.0 + jnp.tanh(0.5 * pre))).astype(jnp.bfloat16)
            estimate = jnp.dot(activated, projection, preferred_element_type=jnp.float32)
            held = noisy_ref[v, f : f + CHUNK]
            target[v, f : f + CHUNK] = (held - level * estimate.reshape(held.shape)).astype(
                jnp.bfloat16
            )

    def convolve(v):
        for d, (axis, step) in enumerate(SIDES):
            @pl.when(has(axis, -step))
            def _():
                edge(d, v).wait_recv()
        number = (v >= videos).astype(jnp.int32) if ahead else 0
        middle[v, 0, 1 : 1 + rows] = edge_in[0, v].astype(jnp.float32).reshape(rows, cols, channels)
        middle[v, frames + 1, 1 : 1 + rows] = (
            edge_in[1, v].astype(jnp.float32).reshape(rows, cols, channels)
        )
        for d, at in ((2, 0), (3, rows + 1)):
            middle[v, 1 : 1 + frames, at] = (
                edge_in[d, v].astype(jnp.float32).reshape(frames, cols, channels)
            )
        estimate_into(result, v, number)

        wholes = jnp.where(first, early, 0)

        @pl.when(jnp.logical_and(turn(v) >= DEPTH + wholes, sends(v)))
        def _():
            sent(turn(v) - DEPTH).wait_send()

        for w in range(early):
            @pl.when(jnp.logical_and(first, v == w))
            def _():
                for n in range(1, PIECES):
                    piece(w, n).start()

        @pl.when(jnp.logical_and(passes(v), v >= wholes))
        def _():
            pass_on(v).start()

        if ahead:
            @pl.when(v >= videos)
            def _():
                finish(v).start()

        @pl.when(v < videos)
        def _():
            out_ref[v] = result[v]

    for copy in weight_loads:
        copy.wait()
    pack(0)

    def start(v):
        load_noise(v).wait()
        load_base(v).wait()
        normalise(v, 0)

    @pl.when(first)
    def _():
        start(0)
        if early:
            estimate_into(inner, 0, 0)

    pl.semaphore_wait(barrier, sum(has(*side).astype(jnp.int32) for side in neighbours))

    @pl.when(first)
    def _():
        send_edges(0)
        if early:
            piece(0, 0).start()
        for v in range(1, early):
            start(v)
            send_edges(v)
            estimate_into(inner, v, 0)
            piece(v, 0).start()

    if ahead:
        @pl.when(later)
        def _():
            for copy in loans:
                copy.start()

    @pl.loop(0, items + 1)
    def _(i):
        @pl.when(jnp.logical_and(active(i), jnp.logical_or(i >= max(early, 1), later)))
        def _():
            prepare(i)
            send_edges(i)

        @pl.when(jnp.logical_and(i > 0, active(i - 1)))
        def _():
            convolve(i - 1)

    @pl.loop(0, items)
    def _(j):
        @pl.when(active(j))
        def _():
            for d, side in enumerate(SIDES):
                @pl.when(has(*side))
                def _():
                    edge(d, j).wait_send()

    if early:
        @pl.when(first)
        def _():
            for v in range(early):
                for n in range(PIECES):
                    piece(v, n).wait_send()

    @pl.when(onward)
    def _():
        for n in range(max(videos - DEPTH, 0), videos):
            sent(n).wait_send()

    if ahead:
        @pl.when(later)
        def _():
            for copy in loans:
                copy.wait_send()
            for j in range(videos, items):
                finish(j).wait_recv()


def on_device(
    base_frames, section_noise, noise_levels, spatial_kernel, temporal_kernel, output_weight
):
    videos, frames, rows, cols, channels = base_frames.shape
    ahead = AHEAD if lax.axis_size("section") == 2 and videos > AHEAD + 1 else 0
    early = EARLY if lax.axis_size("section") > 1 and videos >= EARLY + DEPTH + ahead else 0
    items = videos + ahead
    flat = (frames, rows * cols, channels)
    edges = (len(SIDES), items, frames * cols, channels)
    assert frames == rows and frames % CHUNK == 0 and MARGIN % cols == 0
    assert rows * cols > 2 * MARGIN and frames > 2
    result = pl.pallas_call(
        functools.partial(kernel, videos, ahead, early, frames, rows, cols, channels),
        out_shape=pltpu.VMEM((videos,) + flat, jnp.bfloat16),
        in_specs=[pl.BlockSpec(memory_space=pltpu.VMEM)] + [pl.BlockSpec(memory_space=pltpu.HBM)] * 5,
        out_specs=pl.BlockSpec(memory_space=pltpu.VMEM),
        scratch_shapes=[
            pltpu.VMEM((items,) + flat, jnp.bfloat16),
            pltpu.VMEM((items,) + flat, jnp.bfloat16),
            pltpu.VMEM((items,) + flat, jnp.bfloat16),
            pltpu.VMEM((1 + ahead, 13, channels, channels), jnp.bfloat16),
            pltpu.VMEM((1 + ahead, 2, 4 * channels, 2 * channels), jnp.bfloat16),
            pltpu.VMEM((1 + ahead, 8, channels), jnp.float32),
            pltpu.VMEM((16, channels), jnp.bfloat16),
            pltpu.VMEM((16, channels), jnp.bfloat16),
            pltpu.VMEM((items,) + flat, jnp.float32),
            pltpu.VMEM((items, frames + 2, rows + 2, cols, channels), jnp.float32),
            pltpu.VMEM(edges, jnp.bfloat16),
            pltpu.VMEM(edges, jnp.bfloat16),
            pltpu.VMEM((EARLY,) + flat, jnp.bfloat16),
            pltpu.SemaphoreType.DMA((videos,)),
            pltpu.SemaphoreType.DMA((videos,)),
            pltpu.SemaphoreType.DMA((3,)),
            pltpu.SemaphoreType.DMA((items,)),
            pltpu.SemaphoreType.DMA((items,)),
            pltpu.SemaphoreType.DMA((len(SIDES), items)),
            pltpu.SemaphoreType.DMA((len(SIDES), items)),
            pltpu.SemaphoreType.DMA((4 + videos,)),
            pltpu.SemaphoreType.DMA((4 + videos,)),
            pltpu.SemaphoreType.DMA((EARLY, PIECES)),
            pltpu.SemaphoreType.DMA((EARLY, PIECES)),
        ],
        compiler_params=pltpu.CompilerParams(
            collective_id=0, has_side_effects=True, vmem_limit_bytes=58 * 2**20
        ),
    )(
        noise_levels.reshape(1, 1),
        base_frames.reshape((videos,) + flat),
        section_noise.reshape((videos,) + flat),
        spatial_kernel[0],
        temporal_kernel[0],
        output_weight,
    )
    return result.reshape((1,) + base_frames.shape)


def solution(mesh):
    return jax.shard_map(
        on_device,
        mesh=mesh,
        in_specs=(
            P(None, "frames", "space", None, None),
            P("section", None, "frames", "space", None, None),
            P("section"),
            P("section", None, None, None),
            P("section", None, None, None),
            P("section", None, None),
        ),
        out_specs=P("section", None, "frames", "space", None, None),
        check_vma=False,
    )
```

```python
import functools

import jax
import jax.numpy as jnp
from jax import lax
from jax.experimental import pallas as pl
from jax.experimental.pallas import tpu as pltpu
from jax.sharding import PartitionSpec as P

MESH = pl.DeviceIdType.MESH
SIDES = (("frames", 1), ("frames", -1), ("space", 1), ("space", -1))
CHUNK = 8
DEPTH = 3
AHEAD = 2
EARLY = 1
MARGIN = 16
PIECES = 5


def kernel(
    videos, ahead, early, frames, rows, cols, channels,
    level_ref, base_hbm, noise_hbm, spatial_hbm, temporal_hbm, output_hbm, out_ref,
    noise, prior, result, weights, packed, levels, level_out, level_in,
    noisy_ref, middle, edge_out, edge_in, inner,
    noise_sem, base_sem, weight_sem, chain_send, chain_recv, edge_send, edge_recv,
    lend_send, lend_recv, piece_send, piece_recv,
):
    place = {axis: lax.axis_index(axis) for axis in ("section", "frames", "space")}
    count = {axis: lax.axis_size(axis) for axis in place}

    around = {
        (axis, step): jnp.clip(place[axis] + step, 0, count[axis] - 1)
        for axis in place
        for step in (1, -1)
    }
    exists = {
        (axis, step): place[axis] < count[axis] - 1 if step > 0 else place[axis] > 0
        for axis, step in around
    }

    def has(axis, step):
        return exists[axis, step]

    def peer(axis, step):
        return {axis: around[axis, step]}

    first = place["section"] == 0
    later = jnp.logical_not(first)
    onward = has("section", 1)
    items = videos + ahead
    lag = ahead + 1

    def special(v):
        return jnp.logical_and(v >= videos - lag, v < videos - 1) if ahead else False

    def active(j):
        if not ahead:
            return j < videos
        usual = jnp.logical_and(j < videos, jnp.logical_not(special(j)))
        return jnp.logical_or(usual, jnp.logical_and(first, j < items))

    def load_noise(v):
        return pltpu.make_async_copy(noise_hbm.at[v], noise.at[v], noise_sem.at[v])

    def load_base(v):
        return pltpu.make_async_copy(base_hbm.at[v], prior.at[v], base_sem.at[v])

    def turn(v):
        return v - ahead * (v >= videos - 1).astype(jnp.int32) if ahead else v

    def sent(n):
        return pltpu.make_async_remote_copy(
            src_ref=result.at[0], dst_ref=prior.at[0],
            send_sem=chain_send.at[n], recv_sem=chain_recv.at[n],
            device_id=peer("section", 1), device_id_type=MESH,
        )

    def pass_on(v):
        return pltpu.make_async_remote_copy(
            src_ref=result.at[v], dst_ref=prior.at[v],
            send_sem=chain_send.at[turn(v)], recv_sem=chain_recv.at[turn(v)],
            device_id=peer("section", 1), device_id_type=MESH,
        )

    def piece(v, n):
        core = pl.ds(MARGIN, rows * cols - 2 * MARGIN)
        part = (
            (pl.ds(1, frames - 2), core),
            (pl.ds(0, frames), pl.ds(0, MARGIN)),
            (pl.ds(0, frames), pl.ds(rows * cols - MARGIN, MARGIN)),
            (pl.ds(0, 1), core),
            (pl.ds(frames - 1, 1), core),
        )[n]
        source = inner if n == 0 else result
        return pltpu.make_async_remote_copy(
            src_ref=source.at[v, part[0], part[1]], dst_ref=prior.at[v, part[0], part[1]],
            send_sem=piece_send.at[v, n], recv_sem=piece_recv.at[v, n],
            device_id=peer("section", 1), device_id_type=MESH,
        )

    def finish(j):
        return pltpu.make_async_remote_copy(
            src_ref=result.at[j], dst_ref=out_ref.at[j - lag],
            send_sem=chain_send.at[j - ahead], recv_sem=chain_recv.at[j - ahead],
            device_id=peer("section", 1), device_id_type=MESH,
        )

    def edge(d, v):
        return pltpu.make_async_remote_copy(
            src_ref=edge_out.at[d, v], dst_ref=edge_in.at[d, v],
            send_sem=edge_send.at[d, v], recv_sem=edge_recv.at[d, v],
            device_id=peer(*SIDES[d]), device_id_type=MESH,
        )

    parts = ((spatial_hbm, 0, 9), (temporal_hbm, 9, 3), (output_hbm, 12, 1))
    weight_loads = [
        pltpu.make_async_copy(source, weights.at[0, pl.ds(at, size)], weight_sem.at[n])
        for n, (source, at, size) in enumerate(parts)
    ]
    loans = []
    if ahead:
        pairs = [(level_out, level_in)]
        pairs += [(source, weights.at[1, pl.ds(at, size)]) for source, at, size in parts]
        for v in range(videos - lag, videos - 1):
            pairs.append((noise_hbm.at[v], noise.at[v + lag]))
        loans = [
            pltpu.make_async_remote_copy(
                src_ref=source, dst_ref=target, send_sem=lend_send.at[n], recv_sem=lend_recv.at[n],
                device_id=peer("section", -1), device_id_type=MESH,
            )
            for n, (source, target) in enumerate(pairs)
        ]

    def passes(v):
        if not ahead:
            return onward
        return jnp.logical_and(onward, jnp.logical_and(v < videos, jnp.logical_not(special(v))))

    def sends(v):
        return jnp.logical_or(passes(v), v >= videos)

    neighbours = SIDES + (("section", 1), ("section", -1))
    barrier = pltpu.get_barrier_semaphore()
    for axis, step in neighbours:
        @pl.when(has(axis, step))
        def _():
            pl.semaphore_signal(barrier, inc=1, device_id=peer(axis, step), device_id_type=MESH)

    @pl.loop(0, videos)
    def _(v):
        @pl.when(active(v))
        def _():
            load_noise(v).start()

        @pl.when(first)
        def _():
            load_base(v).start()

    for copy in weight_loads:
        copy.start()

    for d, (axis, step) in enumerate(SIDES):
        @pl.when(jnp.logical_not(has(axis, -step)))
        def _():
            edge_in[d] = jnp.zeros(edge_in.shape[1:], edge_in.dtype)

    levels[0] = jnp.broadcast_to(level_ref[...].astype(jnp.float32), levels.shape[1:])
    level_out[...] = jnp.broadcast_to(level_ref[...], level_out.shape)

    def pack(number):
        packed[number] = jnp.zeros(packed.shape[1:], packed.dtype)
        for a in range(3):
            line = pl.ds(a * channels, channels)
            packed[number, 0, line, :channels] = weights[number, 3 * a + 1]
            packed[number, 0, line, channels:] = weights[number, 3 * a + 2]
            packed[number, 1, line, :channels] = weights[number, 3 * a]
        packed[number, 0, 3 * channels :, :channels] = weights[number, 9]
        packed[number, 1, channels : 2 * channels, channels:] = weights[number, 10]
        packed[number, 1, 3 * channels :, channels:] = weights[number, 11]

    def normalise(v, number):
        noisy = prior[v].astype(jnp.float32) + levels[number][0:1] * noise[v].astype(jnp.float32)
        noisy_ref[v] = noisy
        power = jnp.mean(noisy * noisy, axis=-1, keepdims=True)
        normalized = (noisy * lax.rsqrt(power + 1e-05)).astype(jnp.bfloat16)
        x = normalized.astype(jnp.float32).reshape(frames, rows, cols, channels)
        edge_out[0, v] = normalized[frames - 1]
        edge_out[1, v] = normalized[0]
        edge_out[2, v] = x[:, rows - 1].reshape(frames * cols, channels).astype(jnp.bfloat16)
        edge_out[3, v] = x[:, 0].reshape(frames * cols, channels).astype(jnp.bfloat16)
        middle[v, 1 : 1 + frames, 1 : 1 + rows] = x

    def send_edges(v):
        for d, side in enumerate(SIDES):
            @pl.when(has(*side))
            def _():
                edge(d, v).start()

    def prepare(i):
        @pl.when(i < videos)
        def _():
            load_noise(i).wait()

            @pl.when(first)
            def _():
                load_base(i).wait()

            if early:
                second = place["section"] == 1
                for v in range(early):
                    @pl.when(jnp.logical_and(second, i == v))
                    def _():
                        for n in range(PIECES):
                            piece(v, n).wait_recv()

                whole = jnp.logical_or(place["section"] > 1, jnp.logical_and(second, i >= early))
            else:
                whole = later

            @pl.when(whole)
            def _():
                pass_on(i).wait_recv()

        if ahead:
            @pl.when(i == videos)
            def _():
                for copy in loans:
                    copy.wait_recv()
                levels[1] = level_in[0:8].astype(jnp.float32)
                pack(1)

            @pl.when(i >= videos)
            def _():
                prior[i] = result[i - lag]

        normalise(i, (i >= videos).astype(jnp.int32) if ahead else 0)

    def estimate_into(target, v, number):
        projection = weights[number, 12]
        level = levels[number][0:1]
        lines = CHUNK * rows
        column = lax.broadcasted_iota(jnp.int32, (lines, cols, channels), 1)
        for f in range(0, frames, CHUNK):
            views = [middle[v, f + 1 : f + 1 + CHUNK, a : a + rows] for a in range(3)]
            views += [middle[v, f + t : f + t + CHUNK, 1 : 1 + rows] for t in (0, 2)]
            views = [view.reshape(-1, channels).astype(jnp.bfloat16) for view in views]
            sums = [
                jnp.dot(
                    jnp.concatenate(views[:3] + [views[3 + n]], axis=-1), packed[number, n],
                    preferred_element_type=jnp.float32,
                )
                for n in range(2)
            ]
            ahead_part = sums[0][:, channels:].reshape(lines, cols, channels)
            behind_part = sums[1][:, :channels].reshape(lines, cols, channels)
            shifted = jnp.where(column == cols - 1, 0.0, pltpu.roll(ahead_part, cols - 1, 1))
            shifted = shifted + jnp.where(column == 0, 0.0, pltpu.roll(behind_part, 1, 1))
            pre = sums[0][:, :channels] + sums[1][:, channels:] + shifted.reshape(-1, channels)
            activated = (0.5 * pre * (1.0 + jnp.tanh(0.5 * pre))).astype(jnp.bfloat16)
            estimate = jnp.dot(activated, projection, preferred_element_type=jnp.float32)
            held = noisy_ref[v, f : f + CHUNK]
            target[v, f : f + CHUNK] = (held - level * estimate.reshape(held.shape)).astype(
                jnp.bfloat16
            )

    def convolve(v):
        for d, (axis, step) in enumerate(SIDES):
            @pl.when(has(axis, -step))
            def _():
                edge(d, v).wait_recv()
        number = (v >= videos).astype(jnp.int32) if ahead else 0
        middle[v, 0, 1 : 1 + rows] = edge_in[0, v].astype(jnp.float32).reshape(rows, cols, channels)
        middle[v, frames + 1, 1 : 1 + rows] = (
            edge_in[1, v].astype(jnp.float32).reshape(rows, cols, channels)
        )
        for d, at in ((2, 0), (3, rows + 1)):
            middle[v, 1 : 1 + frames, at] = (
                edge_in[d, v].astype(jnp.float32).reshape(frames, cols, channels)
            )
        estimate_into(result, v, number)

        wholes = jnp.where(first, early, 0)

        @pl.when(jnp.logical_and(turn(v) >= DEPTH + wholes, sends(v)))
        def _():
            sent(turn(v) - DEPTH).wait_send()

        for w in range(early):
            @pl.when(jnp.logical_and(first, v == w))
            def _():
                for n in range(1, PIECES):
                    piece(w, n).start()

        @pl.when(jnp.logical_and(passes(v), v >= wholes))
        def _():
            pass_on(v).start()

        if ahead:
            @pl.when(v >= videos)
            def _():
                finish(v).start()

        @pl.when(v < videos)
        def _():
            out_ref[v] = result[v]

    for copy in weight_loads:
        copy.wait()
    pack(0)

    def start(v):
        load_noise(v).wait()
        load_base(v).wait()
        normalise(v, 0)

    @pl.when(first)
    def _():
        start(0)
        if early:
            estimate_into(inner, 0, 0)

    pl.semaphore_wait(barrier, sum(has(*side).astype(jnp.int32) for side in neighbours))

    @pl.when(first)
    def _():
        send_edges(0)
        if early:
            piece(0, 0).start()
        for v in range(1, early):
            start(v)
            send_edges(v)
            estimate_into(inner, v, 0)
            piece(v, 0).start()

    if ahead:
        @pl.when(later)
        def _():
            for copy in loans:
                copy.start()

    @pl.loop(0, items + 1)
    def _(i):
        @pl.when(jnp.logical_and(active(i), jnp.logical_or(i >= max(early, 1), later)))
        def _():
            prepare(i)
            send_edges(i)

        @pl.when(jnp.logical_and(i > 0, active(i - 1)))
        def _():
            convolve(i - 1)

    @pl.loop(0, items)
    def _(j):
        @pl.when(active(j))
        def _():
            for d, side in enumerate(SIDES):
                @pl.when(has(*side))
                def _():
                    edge(d, j).wait_send()

    if early:
        @pl.when(first)
        def _():
            for v in range(early):
                for n in range(PIECES):
                    piece(v, n).wait_send()

    @pl.when(onward)
    def _():
        for n in range(max(videos - DEPTH, 0), videos):
            sent(n).wait_send()

    if ahead:
        @pl.when(later)
        def _():
            for copy in loans:
                copy.wait_send()
            for j in range(videos, items):
                finish(j).wait_recv()


def on_device(
    base_frames, section_noise, noise_levels, spatial_kernel, temporal_kernel, output_weight
):
    videos, frames, rows, cols, channels = base_frames.shape
    ahead = AHEAD if lax.axis_size("section") == 2 and videos > AHEAD + 1 else 0
    early = EARLY if lax.axis_size("section") > 1 and videos >= EARLY + DEPTH + ahead else 0
    items = videos + ahead
    flat = (frames, rows * cols, channels)
    edges = (len(SIDES), items, frames * cols, channels)
    assert frames == rows and frames % CHUNK == 0 and MARGIN % cols == 0
    assert rows * cols > 2 * MARGIN and frames > 2
    result = pl.pallas_call(
        functools.partial(kernel, videos, ahead, early, frames, rows, cols, channels),
        out_shape=pltpu.VMEM((videos,) + flat, jnp.bfloat16),
        in_specs=[pl.BlockSpec(memory_space=pltpu.VMEM)] + [pl.BlockSpec(memory_space=pltpu.HBM)] * 5,
        out_specs=pl.BlockSpec(memory_space=pltpu.VMEM),
        scratch_shapes=[
            pltpu.VMEM((items,) + flat, jnp.bfloat16),
            pltpu.VMEM((items,) + flat, jnp.bfloat16),
            pltpu.VMEM((items,) + flat, jnp.bfloat16),
            pltpu.VMEM((1 + ahead, 13, channels, channels), jnp.bfloat16),
            pltpu.VMEM((1 + ahead, 2, 4 * channels, 2 * channels), jnp.bfloat16),
            pltpu.VMEM((1 + ahead, 8, channels), jnp.float32),
            pltpu.VMEM((16, channels), jnp.bfloat16),
            pltpu.VMEM((16, channels), jnp.bfloat16),
            pltpu.VMEM((items,) + flat, jnp.float32),
            pltpu.VMEM((items, frames + 2, rows + 2, cols, channels), jnp.float32),
            pltpu.VMEM(edges, jnp.bfloat16),
            pltpu.VMEM(edges, jnp.bfloat16),
            pltpu.VMEM((EARLY,) + flat, jnp.bfloat16),
            pltpu.SemaphoreType.DMA((videos,)),
            pltpu.SemaphoreType.DMA((videos,)),
            pltpu.SemaphoreType.DMA((3,)),
            pltpu.SemaphoreType.DMA((items,)),
            pltpu.SemaphoreType.DMA((items,)),
            pltpu.SemaphoreType.DMA((len(SIDES), items)),
            pltpu.SemaphoreType.DMA((len(SIDES), items)),
            pltpu.SemaphoreType.DMA((4 + videos,)),
            pltpu.SemaphoreType.DMA((4 + videos,)),
            pltpu.SemaphoreType.DMA((EARLY, PIECES)),
            pltpu.SemaphoreType.DMA((EARLY, PIECES)),
        ],
        compiler_params=pltpu.CompilerParams(
            collective_id=0, has_side_effects=True, vmem_limit_bytes=58 * 2**20
        ),
    )(
        noise_levels.reshape(1, 1),
        base_frames.reshape((videos,) + flat),
        section_noise.reshape((videos,) + flat),
        spatial_kernel[0],
        temporal_kernel[0],
        output_weight,
    )
    return result.reshape((1,) + base_frames.shape)


def solution(mesh):
    return jax.shard_map(
        on_device,
        mesh=mesh,
        in_specs=(
            P(None, "frames", "space", None, None),
            P("section", None, "frames", "space", None, None),
            P("section"),
            P("section", None, None, None),
            P("section", None, None, None),
            P("section", None, None),
        ),
        out_specs=P("section", None, "frames", "space", None, None),
        check_vma=False,
    )
```
